32 devices in a mesh: dp: 16 (over z, x, core), mp: 2 (over y).
Axes of the slice: x: 2, y: 2, z: 4, core: 2. Of those that a mesh axis runs over, the one named last changes fastest.
Arguments:
- tokens: bfloat16 [147456, 512], P(('dp', 'mp')), may hold values from -6 to 6
- cotangent: bfloat16 [147456, 512], P(('dp', 'mp')), may hold values from -6 to 6
- frame_count: int32 [3072], P('dp'), may hold values from 1 to 6
- live_count: int32 [16], P('dp'), may hold values from 1 to 192, as said below
- w_query: bfloat16 [512, 512], P('dp', 'mp'), may hold values from -0.25 to 0.25
- w_key: bfloat16 [512, 512], P('dp', 'mp'), may hold values from -0.25 to 0.25
- w_value: bfloat16 [512, 512], P('dp', 'mp'), may hold values from -0.25 to 0.25
- w_out: bfloat16 [512, 512], P('mp', 'dp'), may hold values from -1 to 1
- w_up: bfloat16 [512, 2048], P('dp', 'mp'), may hold values from -0.25 to 0.25
- w_down: bfloat16 [2048, 512], P('mp', 'dp'), may hold values from -0.1875 to 0.1875
- gain_one: bfloat16 [512], P('dp'), may hold values from 0.5 to 1.5
- shift_one: bfloat16 [512], P('dp'), may hold values from -4 to 4
- gain_two: bfloat16 [512], P('dp'), may hold values from 0.5 to 1.5
- shift_two: bfloat16 [512], P('dp'), may hold values from -4 to 4
Outputs:
- mixed: bfloat16 [147456, 512], P(('dp', 'mp'))
- grad_input: float32 [147456, 512], P(('dp', 'mp'))
- grad_w_query: float32 [512, 512], P('dp', 'mp')
- grad_w_key: float32 [512, 512], P('dp', 'mp')
- grad_w_value: float32 [512, 512], P('dp', 'mp')
- grad_w_out: float32 [512, 512], P('mp', 'dp')
- grad_w_up: float32 [512, 2048], P('dp', 'mp')
- grad_w_down: float32 [2048, 512], P('mp', 'dp')
- grad_gain_one: float32 [512], P('dp')
- grad_shift_one: float32 [512], P('dp')
- grad_gain_two: float32 [512], P('dp')
- grad_shift_two: float32 [512], P('dp')
The draws below stay inside these ranges and needn't reach their ends.
Inputs may be any that keep to these rules, and one draw needn't show every extreme that they name: The first live_count[d] sequence slots of data group d are live, the rest are padding; in every draw some group has all 192 slots live. The first frame_count[s] frames of slot s are valid keys.
All inputs are finite; a program needn't handle non-finite values.
Results may differ from the reference program's by a relative error of at most 0.012.
Values may be sent and summed in bfloat16 or wider, within the bound.
No kernel may reach another device: no remote copies, remote signals or barrier semaphores. Data moves between devices by JAX's collectives and lax.ppermute only.
A program may use at most 384 MiB of HBM per device.

```python
import jax
import jax.numpy as jnp
from jax import lax

D = 512
HEADS = 8
HEAD = 64
FF = 2048
FRAMES = 6
FTOK = 8
SEQLEN = 48
SEQ_DEV = 192
SEQS = 3072
TOKENS = 147456
N_DP = 16


def draw_live_count(key, part):
    key = jax.random.fold_in(key, 7)
    first, second = jax.random.split(key)
    level = jax.random.randint(first, (N_DP,), 1, 9)
    counts = jnp.maximum(SEQ_DEV * level * level // 64, 1)
    full_group = jax.random.randint(second, (), 0, N_DP)
    counts = jnp.where(jnp.arange(N_DP) == full_group, SEQ_DEV, counts)
    return counts.astype(jnp.int32)


def with_ends(result, key, low, top_value):
    extent = result.shape
    place = [jax.random.randint(jax.random.fold_in(key, axis), (), 0, extent[axis]) for axis in range(len(extent))]
    result = result.at[tuple(place)].set(low)
    longest = extent.index(max(extent))
    place[longest] = (place[longest] + 1) % extent[longest]
    return result.at[tuple(place)].set(top_value)


def levels(key, extent, cuts, smallest, largest):
    loudness, own = 1.0, jax.random.fold_in(key, 6)
    for dim, shards_of in cuts:
        heights = jnp.exp(jax.random.uniform(jax.random.fold_in(own, dim), (shards_of,), jnp.float32, smallest / len(cuts), largest / len(cuts)))
        loudness = loudness * jnp.repeat(heights, extent[dim] // shards_of).reshape([-1 if axis == dim else 1 for axis in range(len(extent))])
    return loudness


def normal_values(key, dims, width, limit, pieces=(), kind=jnp.bfloat16):
    entries = jax.random.normal(key, dims, jnp.float32) * width
    if len(pieces) > 0:
        entries = levels(key, dims, pieces, -0.22, 0.18) * entries
    return jnp.clip(entries, min=-limit, max=limit).astype(kind)


def setup_inputs(seed: int = 0) -> dict:
    seeds = jax.random.split(jax.random.key(seed), 15)
    return {
        "tokens": normal_values(seeds[0], (TOKENS, D), 1.0, 6.0, ((0, 32),)),
        "cotangent": normal_values(seeds[1], (TOKENS, D), 1.0, 6.0, ((0, 32),)),
        "frame_count": with_ends(jax.random.randint(seeds[2], (SEQS,), 1, FRAMES + 1), jax.random.fold_in(seeds[2], 1), 1, FRAMES).astype(jnp.int32),
        "live_count": draw_live_count(jax.random.fold_in(seeds[14], 71), 0),
        "w_query": normal_values(seeds[4], (D, HEADS * HEAD), D ** -0.5, 0.25, ((0, 16), (1, 2))),
        "w_key": normal_values(seeds[5], (D, HEADS * HEAD), D ** -0.5, 0.25, ((0, 16), (1, 2))),
        "w_value": normal_values(seeds[6], (D, HEADS * HEAD), D ** -0.5, 0.25, ((0, 16), (1, 2))),
        "w_out": normal_values(seeds[7], (HEADS * HEAD, D), (HEADS * HEAD // 16) ** -0.5, 1.0, ((0, 2), (1, 16))),
        "w_up": normal_values(seeds[8], (D, FF), D ** -0.5, 0.25, ((0, 16), (1, 2))),
        "w_down": normal_values(seeds[9], (FF, D), (FF // 2) ** -0.5, 0.1875, ((0, 2), (1, 16))),
        "gain_one": jnp.clip(1.0 + 0.1 * jax.random.normal(seeds[10], (D,), jnp.float32), 0.5, 1.5).astype(jnp.bfloat16),
        "shift_one": normal_values(seeds[11], (D,), 0.4, 4.0, ((0, 16),)),
        "gain_two": jnp.clip(1.0 + 0.1 * jax.random.normal(seeds[12], (D,), jnp.float32), 0.5, 1.5).astype(jnp.bfloat16),
        "shift_two": normal_values(seeds[13], (D,), 0.4, 4.0, ((0, 16),)),
    }


@jax.custom_vjp
def low(v):
    return lax.optimization_barrier(v.astype(jnp.bfloat16)).astype(jnp.float32)

@jax.custom_vjp
def low_back(v):
    return v

def low_keep(v):
    return (low(v), None)

def low_pass(kept, grad):
    return (grad,)

def back_keep(v):
    return (v, None)

def back_low(kept, grad):
    return (low(grad),)
low.defvjp(low_keep, low_pass)
low_back.defvjp(back_keep, back_low)
EPS = 1e-05
HIGH = lax.Precision.HIGHEST

def rounded_both(value):
    return low(low_back(value))

def layer_norm(rows, gain, shift):
    mean = lax.optimization_barrier(jnp.mean(rows, axis=-1, keepdims=True))
    centered = rows - mean
    spread = lax.optimization_barrier(jnp.mean(centered * centered, axis=-1, keepdims=True))
    return centered * lax.rsqrt(spread + EPS) * gain + shift

def key_mask(frame_count, seqlen, ftok):
    places = jnp.arange(seqlen, dtype=jnp.int32)
    causal = places[None, :] <= places[:, None]
    valid = (places // ftok)[None, :] < frame_count[:, None]
    return causal[None, None, :, :] & valid[:, None, None, :]

def block_forward(rows, weights, frame_count):
    w_query, w_key, w_value, w_out, w_up, w_down, gain_one, shift_one, gain_two, shift_two = weights
    count = rows.shape[0] // SEQLEN
    normed = low(layer_norm(rows, gain_one, shift_one))

    def split_heads(value):
        return value.reshape(count, SEQLEN, HEADS, HEAD)
    query = split_heads(rounded_both(jnp.dot(normed, w_query, precision=HIGH)))
    keys = split_heads(rounded_both(jnp.dot(normed, w_key, precision=HIGH)))
    values = split_heads(rounded_both(jnp.dot(normed, w_value, precision=HIGH)))
    scale = HEAD ** (-0.5)
    scores = low_back(jnp.einsum('sqhe,skhe->shqk', query, keys, precision=HIGH) * scale)
    scores = jnp.where(key_mask(frame_count, SEQLEN, FTOK), scores, -1000000000.0)
    top = lax.optimization_barrier(jnp.max(scores, axis=-1, keepdims=True))
    expd = jnp.exp(scores - top)
    probs = expd / lax.optimization_barrier(jnp.sum(expd, axis=-1, keepdims=True))
    heads_out = jnp.einsum('shqk,skhe->sqhe', low(probs), values, precision=HIGH)
    heads_out = rounded_both(heads_out.reshape(rows.shape[0], HEADS * HEAD))
    attended = low_back(jnp.dot(heads_out, w_out, precision=HIGH))
    hidden = rows + attended
    normed_two = low(layer_norm(hidden, gain_two, shift_two))
    up_value = low_back(jnp.dot(normed_two, w_up, precision=HIGH))
    act = low(jax.nn.gelu(up_value))
    down = low_back(jnp.dot(act, w_down, precision=HIGH))
    return hidden + down

def reference(tokens, cotangent, frame_count, live_count, w_query, w_key, w_value, w_out, w_up, w_down, gain_one, shift_one, gain_two, shift_two):
    weights = tuple((w.astype(jnp.float32) for w in (w_query, w_key, w_value, w_out, w_up, w_down, gain_one, shift_one, gain_two, shift_two)))
    group_rows = SEQ_DEV * SEQLEN
    rows = tokens.astype(jnp.float32).reshape(N_DP, group_rows, D)
    cots = cotangent.astype(jnp.float32).reshape(N_DP, group_rows, D)
    counts = frame_count.reshape(N_DP, SEQ_DEV)
    slot_of_row = jnp.arange(group_rows, dtype=jnp.int32) // SEQLEN

    def step(totals, item):
        group_in, group_cot, group_frames, group_live = item
        outputs, pull = jax.vjp(lambda xs, ws: block_forward(xs, ws, group_frames), group_in, weights)
        live = (slot_of_row < group_live).astype(jnp.float32)[:, None]
        grad_rows, grad_weights = pull(group_cot * live)
        totals = jax.tree.map(lambda a, b: a + b, totals, grad_weights)
        return (totals, (outputs, grad_rows))
    start = tuple((jnp.zeros_like(w) for w in weights))
    totals, (outputs, grads) = lax.scan(step, start, (rows, cots, counts, live_count))
    mixed = outputs.reshape(TOKENS, D).astype(jnp.bfloat16)
    grad_input = grads.reshape(TOKENS, D)
    return (mixed, grad_input, totals[0], totals[1], totals[2], totals[3], totals[4], totals[5], totals[6], totals[7], totals[8], totals[9])
```

```python
import jax
import jax.numpy as jnp
from jax import lax
from jax.experimental import pallas as pl
from jax.experimental.pallas import tpu as pltpu
from jax.sharding import PartitionSpec as P

D = 512
FF = 2048
HEAD = 64
FTOK = 8
SEQ = 48
HALVES = 2
HW = D // HALVES
FW = FF // HALVES
GC = 128
EPS = 1e-05
SEQS_STEP = 8
ROWS = SEQS_STEP * SEQ
BF = jnp.bfloat16
F32 = jnp.float32


def nn(a, b):
    return lax.dot_general(a, b, (((1,), (0,)), ((), ())), preferred_element_type=F32)


def nt(a, b):
    return lax.dot_general(a, b, (((1,), (1,)), ((), ())), preferred_element_type=F32)


def tn(a, b):
    return lax.dot_general(a, b, (((0,), (0,)), ((), ())), preferred_element_type=F32)


def norm_parts(rows):
    mean = jnp.mean(rows, axis=-1, keepdims=True)
    centered = rows - mean
    spread = jnp.mean(centered * centered, axis=-1, keepdims=True)
    rstd = lax.rsqrt(spread + EPS)
    return centered * rstd, rstd


def norm_back(n, rstd, gain, gy):
    gg = gy * gain
    first = jnp.mean(gg, axis=-1, keepdims=True)
    second = jnp.mean(gg * n, axis=-1, keepdims=True)
    return rstd * (gg - first - n * second)


def fold_rows(value):
    return jnp.sum(value.reshape(value.shape[0] // 8, 8, value.shape[1]), axis=0)


def per_head(rows):
    width = rows.shape[1]
    lane = lax.broadcasted_iota(jnp.int32, rows.shape, 1) // HEAD
    pad = jnp.zeros((HEAD - SEQ, width), rows.dtype)
    parts = []
    for h in range(width // HEAD):
        parts.append(jnp.where(lane == h, rows, jnp.zeros_like(rows)))
        parts.append(pad)
    return jnp.concatenate(parts, axis=0)


def pair_blocks(product):
    lane = lax.broadcasted_iota(jnp.int32, (SEQ, 2 * HEAD), 1)
    return jnp.where(lane < HEAD, product[:SEQ], product[HEAD : HEAD + SEQ])


def seq_slice(s, c, width):
    return (slice(s * SEQ, (s + 1) * SEQ), slice(c * width, (c + 1) * width))


def attn_forward_kernel(
    frames, x_ref, wa_ref, vec_ref, q_ref, k_ref, v_ref, p_ref, ho_ref, hidden_ref, s_ref
):
    step = pl.program_id(0)
    x = x_ref[...].astype(F32)
    n, _ = norm_parts(x)
    normed = (n * vec_ref[0:1] + vec_ref[1:2]).astype(BF)
    for m in range(HALVES):
        qkv = nn(normed, wa_ref[m, :, : 3 * HW]).astype(BF)
        cols = slice(m * HW, (m + 1) * HW)
        q_ref[:, cols] = qkv[:, :HW]
        k_ref[:, cols] = qkv[:, HW : 2 * HW]
        v_ref[:, cols] = qkv[:, 2 * HW :]
    for s in range(SEQS_STEP):
        for m in range(HALVES):
            at = seq_slice(s, m, HW)
            s_ref[at] = nt(k_ref[at], per_head(q_ref[at]))
    key = lax.broadcasted_iota(jnp.int32, (SEQ, 2 * HEAD), 0)
    query = lax.broadcasted_iota(jnp.int32, (SEQ, 2 * HEAD), 1) % HEAD
    for s in range(SEQS_STEP):
        allowed = (key <= query) & (key < frames[step * SEQS_STEP + s] * FTOK)
        for c in range(D // (2 * HEAD)):
            at = seq_slice(s, c, 2 * HEAD)
            scores = jnp.where(allowed, s_ref[at] * HEAD**-0.5, -1000000000.0)
            expd = jnp.exp(scores - jnp.max(scores, axis=0, keepdims=True))
            p_ref[at] = (expd * (1.0 / jnp.sum(expd, axis=0, keepdims=True))).astype(BF)
    for s in range(SEQS_STEP):
        for c in range(D // (2 * HEAD)):
            at = seq_slice(s, c, 2 * HEAD)
            ho_ref[at] = pair_blocks(tn(p_ref[at], v_ref[at])).astype(BF)
    attended = nt(ho_ref[:, :HW], wa_ref[0, :, 3 * HW : 4 * HW])
    attended += nt(ho_ref[:, HW:], wa_ref[1, :, 3 * HW : 4 * HW])
    hidden_ref[...] = x + attended


GELU_A = (2.0 / jnp.pi) ** 0.5
GELU_B = 0.044715


def feed_forward_kernel(
    live, hidden_ref, cot_ref, wf_ref, vec_ref, mixed_ref, gh_ref, gf_ref, gv_ref,
    acc_ref, gvacc_ref, act_ref, gup_ref, go_ref,
):
    step = pl.program_id(0)
    last = pl.num_programs(0) - 1

    @pl.when(step == 0)
    def _():
        acc_ref[...] = jnp.zeros_like(acc_ref)
        gvacc_ref[...] = jnp.zeros_like(gvacc_ref)

    hidden = hidden_ref[...]
    n, rstd = norm_parts(hidden)
    normed = (n * vec_ref[2:3] + vec_ref[3:4]).astype(BF)
    row = lax.broadcasted_iota(jnp.int32, (ROWS, 1), 0) + step * ROWS
    go = jnp.where(row < live[0] * SEQ, cot_ref[...].astype(F32), 0.0)
    go_ref[...] = go.astype(BF)
    for m in range(HALVES):
        cols = slice(m * FW, (m + 1) * FW)
        up = nn(normed, wf_ref[m, :, :FW])
        ga = nn(go_ref[...], wf_ref[m, :, FW:])
        sq = up * up
        th = jnp.tanh(up * (GELU_A + (GELU_A * GELU_B) * sq))
        half = 0.5 + 0.5 * th
        act_ref[:, cols] = (up * half).astype(BF)
        slope = half + (0.5 * up) * (1.0 - th * th) * (GELU_A + (3.0 * GELU_A * GELU_B) * sq)
        gup_ref[:, cols] = (ga * slope).astype(BF)
    down = jnp.zeros((ROWS, D), F32)
    gy = jnp.zeros((ROWS, D), F32)
    for m in range(HALVES):
        cols = slice(m * FW, (m + 1) * FW)
        down += nt(act_ref[:, cols], wf_ref[m, :, FW:])
        gy += nt(gup_ref[:, cols], wf_ref[m, :, :FW])
        acc_ref[m, :, :FW] += tn(normed, gup_ref[:, cols])
        acc_ref[m, :, FW:] += tn(go_ref[...], act_ref[:, cols])
    mixed_ref[...] = (hidden + down).astype(BF)
    gh_ref[...] = go + norm_back(n, rstd, vec_ref[2:3], gy)
    gvacc_ref[0] += fold_rows(gy * n)
    gvacc_ref[1] += fold_rows(gy)

    @pl.when(step == last)
    def _():
        gf_ref[...] = acc_ref[...].astype(BF)
        gv_ref[0:1] = jnp.sum(gvacc_ref[0], axis=0, keepdims=True)
        gv_ref[1:2] = jnp.sum(gvacc_ref[1], axis=0, keepdims=True)


def attn_backward_kernel(
    x_ref, gh_ref, q_ref, k_ref, v_ref, p_ref, ho_ref, wa_ref, vec_ref, gi_ref, ga_ref, gv_ref,
    acc_ref, gvacc_ref, s_ref, ds_ref, dh_ref, dqkv_ref,
):
    step = pl.program_id(0)
    last = pl.num_programs(0) - 1

    @pl.when(step == 0)
    def _():
        acc_ref[...] = jnp.zeros_like(acc_ref)
        gvacc_ref[...] = jnp.zeros_like(gvacc_ref)

    x = x_ref[...].astype(F32)
    n, rstd = norm_parts(x)
    normed = (n * vec_ref[0:1] + vec_ref[1:2]).astype(BF)
    gh = gh_ref[...]
    gat = gh.astype(BF)
    for m in range(HALVES):
        cols = slice(m * HW, (m + 1) * HW)
        wo = slice(3 * HW, 4 * HW)
        dh_ref[:, cols] = nn(gat, wa_ref[m, :, wo]).astype(BF)
        acc_ref[m, :, wo] += tn(gat, ho_ref[:, cols])
    for s in range(SEQS_STEP):
        for m in range(HALVES):
            at = seq_slice(s, m, HW)
            s_ref[at] = nt(v_ref[at], per_head(dh_ref[at]))
    for s in range(SEQS_STEP):
        for c in range(D // (2 * HEAD)):
            at = seq_slice(s, c, 2 * HEAD)
            probs = p_ref[at].astype(F32)
            gp = s_ref[at]
            delta = jnp.sum(probs * gp, axis=0, keepdims=True)
            ds_ref[at] = (probs * ((gp - delta) * HEAD**-0.5)).astype(BF)
    for s in range(SEQS_STEP):
        for m in range(HALVES):
            at = seq_slice(s, m, HW)
            rows = at[0]
            base = 3 * HW * m
            dqkv_ref[rows, base + 2 * HW : base + 3 * HW] = nn(p_ref[at], per_head(dh_ref[at])).astype(BF)
            dqkv_ref[rows, base + HW : base + 2 * HW] = nn(ds_ref[at], per_head(q_ref[at])).astype(BF)
    for s in range(SEQS_STEP):
        for c in range(D // (2 * HEAD)):
            at = seq_slice(s, c, 2 * HEAD)
            base = 3 * HW * (c // 2) + 2 * HEAD * (c % 2)
            dqkv_ref[at[0], base : base + 2 * HEAD] = pair_blocks(tn(ds_ref[at], k_ref[at])).astype(BF)
    gy = jnp.zeros((ROWS, D), F32)
    for m in range(HALVES):
        cols = slice(3 * HW * m, 3 * HW * (m + 1))
        gy += nt(dqkv_ref[:, cols], wa_ref[m, :, : 3 * HW])
        acc_ref[m, :, : 3 * HW] += tn(normed, dqkv_ref[:, cols])
    gi_ref[...] = gh + norm_back(n, rstd, vec_ref[0:1], gy)
    gvacc_ref[0] += fold_rows(gy * n)
    gvacc_ref[1] += fold_rows(gy)

    @pl.when(step == last)
    def _():
        ga_ref[...] = acc_ref[...].astype(BF)
        gv_ref[0:1] = jnp.sum(gvacc_ref[0], axis=0, keepdims=True)
        gv_ref[1:2] = jnp.sum(gvacc_ref[1], axis=0, keepdims=True)


def row_block(width):
    return pl.BlockSpec((ROWS, width), lambda i, *_: (i, 0))


def held(shape):
    return pl.BlockSpec(shape, lambda i, *_: (0,) * len(shape), pipeline_mode=pl.Buffered(1))


def shape(dims, dtype):
    return jax.ShapeDtypeStruct(dims, dtype)


PARAMS = pltpu.CompilerParams(vmem_limit_bytes=56 * 1024 * 1024)


def attn_forward(frames, tokens, wa, vec):
    rows = tokens.shape[0]
    return pl.pallas_call(
        attn_forward_kernel,
        grid_spec=pltpu.PrefetchScalarGridSpec(
            num_scalar_prefetch=1,
            grid=(rows // ROWS,),
            in_specs=[row_block(D), held(wa.shape), held(vec.shape)],
            out_specs=[row_block(D)] * 6,
            scratch_shapes=[pltpu.VMEM((ROWS, D), F32)],
        ),
        out_shape=[shape((rows, D), BF)] * 5 + [shape((rows, D), F32)],
        compiler_params=PARAMS,
        name="attn_forward",
    )(frames, tokens, wa, vec)


def feed_forward(live, hidden, cotangent, wf, vec):
    rows = hidden.shape[0]
    return pl.pallas_call(
        feed_forward_kernel,
        grid_spec=pltpu.PrefetchScalarGridSpec(
            num_scalar_prefetch=1,
            grid=(rows // ROWS,),
            in_specs=[row_block(D), row_block(D), held(wf.shape), held(vec.shape)],
            out_specs=[row_block(D), row_block(D), held(wf.shape), held((2, D))],
            scratch_shapes=[
                pltpu.VMEM(wf.shape, F32),
                pltpu.VMEM((2, 8, D), F32),
                pltpu.VMEM((ROWS, FF), BF),
                pltpu.VMEM((ROWS, FF), BF),
                pltpu.VMEM((ROWS, D), BF),
            ],
        ),
        out_shape=[
            shape((rows, D), BF),
            shape((rows, D), F32),
            shape(wf.shape, BF),
            shape((2, D), F32),
        ],
        compiler_params=PARAMS,
        name="feed_forward",
    )(live, hidden, cotangent, wf, vec)


def attn_backward(tokens, gh, q, k, v, p, ho, wa, vec):
    rows = tokens.shape[0]
    return pl.pallas_call(
        attn_backward_kernel,
        grid=(rows // ROWS,),
        in_specs=[row_block(D)] * 7 + [held(wa.shape), held(vec.shape)],
        out_specs=[row_block(D), held(wa.shape), held((2, D))],
        scratch_shapes=[
            pltpu.VMEM(wa.shape, F32),
            pltpu.VMEM((2, 8, D), F32),
            pltpu.VMEM((ROWS, D), F32),
            pltpu.VMEM((ROWS, D), BF),
            pltpu.VMEM((ROWS, D), BF),
            pltpu.VMEM((ROWS, 3 * D), BF),
        ],
        out_shape=[shape((rows, D), F32), shape(wa.shape, BF), shape((2, D), F32)],
        compiler_params=PARAMS,
        name="attn_backward",
    )(tokens, gh, q, k, v, p, ho, wa, vec)


def merge_parts(gathered, parts):
    mp, depth, columns = gathered.shape
    if mp == HALVES:
        return gathered
    width = columns // parts
    split = gathered.reshape(HALVES, mp // HALVES, depth, parts, width)
    return split.transpose(0, 2, 3, 1, 4).reshape(HALVES, depth, -1)


def split_parts(whole, parts, mp):
    if mp == HALVES:
        return whole
    depth = whole.shape[1]
    split = whole.reshape(HALVES, depth, parts, mp // HALVES, -1)
    return split.transpose(0, 3, 1, 2, 4).reshape(mp, depth, -1)


def build(mesh):
    n_dp, n_mp = mesh.shape["dp"], mesh.shape["mp"]

    def gather(block):
        out = lax.all_gather(block, ("mp", "dp"), axis=0, tiled=True)
        return out.reshape(n_mp, n_dp * block.shape[0], block.shape[1])

    def scatter(whole):
        flat = whole.reshape(-1, whole.shape[-1])
        return lax.psum_scatter(flat, ("mp", "dp"), scatter_dimension=0, tiled=True)

    def shards(
        tokens, cotangent, frame_count, live_count, w_query, w_key, w_value, w_out, w_up, w_down,
        gain_one, shift_one, gain_two, shift_two,
    ):
        place = lax.axis_index("mp")
        seqs = tokens.shape[0] // SEQ
        frames = lax.dynamic_slice(frame_count, (place * seqs,), (seqs,))
        live = live_count - place * seqs
        vec = jnp.stack([gain_one, shift_one, gain_two, shift_two], axis=1)
        depth = vec.shape[0]
        vec = jnp.pad(vec, ((0, 0), (0, GC - 4)))
        own_a = jnp.concatenate([w_query, w_key, w_value, w_out.T, vec], axis=1)
        own_f = jnp.concatenate([w_up, w_down.T], axis=1)
        got_a = gather(own_a)
        vec = got_a[0, :, -GC:-GC + 4].T.astype(F32)
        wa = merge_parts(got_a[:, :, :-GC], 4)
        wf = merge_parts(gather(own_f), 2)
        q, k, v, p, ho, hidden = attn_forward(frames, tokens, wa, vec)
        mixed, gh, gf, gv_two = feed_forward(live, hidden, cotangent, wf, vec)
        grad_input, ga, gv_one = attn_backward(tokens, gh, q, k, v, p, ho, wa, vec)
        gvec = jnp.concatenate([gv_one, gv_two], axis=0).T.astype(BF)
        gvec = jnp.broadcast_to(jnp.pad(gvec, ((0, 0), (0, GC - 4))), (n_mp, D, GC))
        gf_own = scatter(split_parts(gf, 2, n_mp)).astype(F32)
        ga_own = scatter(jnp.concatenate([split_parts(ga, 4, n_mp), gvec], axis=2)).astype(F32)
        wide = w_query.shape[1]
        tall = w_up.shape[1]
        gains = ga_own[:, 4 * wide :]
        return (
            mixed,
            grad_input,
            ga_own[:, :wide],
            ga_own[:, wide : 2 * wide],
            ga_own[:, 2 * wide : 3 * wide],
            ga_own[:, 3 * wide : 4 * wide].T,
            gf_own[:, :tall],
            gf_own[:, tall:].T,
            gains[:, 0],
            gains[:, 1],
            gains[:, 2],
            gains[:, 3],
        )

    return shards


def solution(mesh):
    rows = P(("dp", "mp"), None)
    wide, tall, dp = P("dp", "mp"), P("mp", "dp"), P("dp")
    return jax.shard_map(
        build(mesh),
        mesh=mesh,
        in_specs=(rows, rows, dp, dp, wide, wide, wide, tall, wide, tall, dp, dp, dp, dp),
        out_specs=(rows, rows, wide, wide, wide, tall, wide, tall, dp, dp, dp, dp),
        check_vma=False,
    )
```

```python
import jax
import jax.numpy as jnp
from jax import lax
from jax.experimental import pallas as pl
from jax.experimental.pallas import tpu as pltpu
from jax.sharding import PartitionSpec as P

D = 512
FF = 2048
HEAD = 64
FTOK = 8
SEQ = 48
HALVES = 2
HW = D // HALVES
FW = FF // HALVES
GC = 128
EPS = 1e-05
SEQS_STEP = 8
ROWS = SEQS_STEP * SEQ
BF = jnp.bfloat16
F32 = jnp.float32


def nn(a, b):
    return lax.dot_general(a, b, (((1,), (0,)), ((), ())), preferred_element_type=F32)


def nt(a, b):
    return lax.dot_general(a, b, (((1,), (1,)), ((), ())), preferred_element_type=F32)


def tn(a, b):
    return lax.dot_general(a, b, (((0,), (0,)), ((), ())), preferred_element_type=F32)


def norm_parts(rows):
    mean = jnp.mean(rows, axis=-1, keepdims=True)
    centered = rows - mean
    spread = jnp.mean(centered * centered, axis=-1, keepdims=True)
    rstd = lax.rsqrt(spread + EPS)
    return centered * rstd, rstd


def norm_back(n, rstd, gain, gy):
    gg = gy * gain
    first = jnp.mean(gg, axis=-1, keepdims=True)
    second = jnp.mean(gg * n, axis=-1, keepdims=True)
    return rstd * (gg - first - n * second)


def fold_rows(value):
    return jnp.sum(value.reshape(value.shape[0] // 8, 8, value.shape[1]), axis=0)


def per_head(rows):
    width = rows.shape[1]
    lane = lax.broadcasted_iota(jnp.int32, rows.shape, 1) // HEAD
    pad = jnp.zeros((HEAD - SEQ, width), rows.dtype)
    parts = []
    for h in range(width // HEAD):
        parts.append(jnp.where(lane == h, rows, jnp.zeros_like(rows)))
        parts.append(pad)
    return jnp.concatenate(parts, axis=0)


def pair_blocks(product):
    lane = lax.broadcasted_iota(jnp.int32, (SEQ, 2 * HEAD), 1)
    return jnp.where(lane < HEAD, product[:SEQ], product[HEAD : HEAD + SEQ])


def seq_slice(s, c, width):
    return (slice(s * SEQ, (s + 1) * SEQ), slice(c * width, (c + 1) * width))


def block_place(place, cr, xr, yr, zr):
    z, x, c, y = place[0], place[1], place[2], place[3]
    z = lax.rem(z - zr + place[4], place[4])
    return (y ^ yr, z * 4 + (x ^ xr) * 2 + (c ^ cr))


def load_pieces(place, pieces, metas, dst, sems):
    copies = []
    for piece, meta in zip(pieces, metas):
        depth = piece.shape[0] // len(meta)
        n_dp = D // depth
        for b, rel in enumerate(meta):
            m, dp = block_place(place, *rel)
            row = pl.multiple_of((m * n_dp + dp) * depth, depth)
            copy = pltpu.make_async_copy(
                piece.at[pl.ds(b * depth, depth), :], dst.at[pl.ds(row, depth), :], sems.at[len(copies)]
            )
            copy.start()
            copies.append(copy)
    return copies


def wait_all(copies):
    for copy in copies:
        copy.wait()


def store_blocks(place, acc, start, own_ref, other_ref):
    slots, n_z, depth, width = own_ref.shape
    n_dp = n_z * 4
    for core in range(2):

        @pl.when(place[2] == core)
        def _():
            for m in range(HALVES):
                for dp in range(n_dp):
                    z, x, c = dp // 4, (dp // 2) % 2, dp % 2
                    slot = (place[1] ^ x) + 2 * (place[3] ^ m)
                    back = lax.rem(z - place[0] + n_z, n_z)
                    rows = slice(dp * depth, (dp + 1) * depth)
                    ref = own_ref if c == core else other_ref
                    ref[slot, back, :, start : start + acc.shape[2]] = acc[m, rows, :].astype(BF)


def attn_scores_kernel(place, frames, metas, x_ref, *refs):
    n = len(metas)
    pieces, (normed_ref, q_ref, k_ref, p_ref, vec_ref, w_ref, s_ref, sems) = refs[:n], refs[n:]
    step = pl.program_id(0)

    @pl.when(step == 0)
    def _():
        wait_all(load_pieces(place, pieces, metas, w_ref, sems))
        vec_ref[...] = w_ref[:D, 2 * HW :].astype(F32).T[:8]

    x = x_ref[...].astype(F32)
    n, _ = norm_parts(x)
    normed = (n * vec_ref[0:1] + vec_ref[1:2]).astype(BF)
    normed_ref[...] = normed
    for m in range(HALVES):
        qk = nn(normed, w_ref[m * D : (m + 1) * D, : 2 * HW]).astype(BF)
        cols = slice(m * HW, (m + 1) * HW)
        q_ref[:, cols] = qk[:, :HW]
        k_ref[:, cols] = qk[:, HW:]
    for s in range(SEQS_STEP):
        for m in range(HALVES):
            at = seq_slice(s, m, HW)
            s_ref[at] = nt(k_ref[at], per_head(q_ref[at]))
    key = lax.broadcasted_iota(jnp.int32, (SEQ, 2 * HEAD), 0)
    query = lax.broadcasted_iota(jnp.int32, (SEQ, 2 * HEAD), 1) % HEAD
    for s in range(SEQS_STEP):
        allowed = (key <= query) & (key < frames[step * SEQS_STEP + s] * FTOK)
        for c in range(D // (2 * HEAD)):
            at = seq_slice(s, c, 2 * HEAD)
            scores = jnp.where(allowed, s_ref[at] * HEAD**-0.5, -1000000000.0)
            expd = jnp.exp(scores - jnp.max(scores, axis=0, keepdims=True))
            p_ref[at] = (expd * (1.0 / jnp.sum(expd, axis=0, keepdims=True))).astype(BF)


def attn_output_kernel(place, metas, x_ref, normed_ref, p_ref, *refs):
    n = len(metas)
    pieces, (v_ref, ho_ref, hidden_ref, w_ref, sems) = refs[:n], refs[n:]

    @pl.when(pl.program_id(0) == 0)
    def _():
        wait_all(load_pieces(place, pieces, metas, w_ref, sems))

    for m in range(HALVES):
        v_ref[:, m * HW : (m + 1) * HW] = nn(normed_ref[...], w_ref[m * D : (m + 1) * D, :HW]).astype(BF)
    for s in range(SEQS_STEP):
        for c in range(D // (2 * HEAD)):
            at = seq_slice(s, c, 2 * HEAD)
            ho_ref[at] = pair_blocks(tn(p_ref[at], v_ref[at])).astype(BF)
    attended = nt(ho_ref[:, :HW], w_ref[:D, HW:]) + nt(ho_ref[:, HW:], w_ref[D:, HW:])
    hidden_ref[...] = x_ref[...].astype(F32) + attended


GELU_A = (2.0 / jnp.pi) ** 0.5
GELU_B = 0.044715


def feed_forward_kernel(place, live, metas_u, metas_d, hidden_ref, cot_ref, vec_ref, *refs):
    n, n_all = len(metas_u), len(metas_u) + len(metas_d)
    (
        mixed_ref, gh_ref, own_ref, other_ref, gv_ref,
        wu_ref, wd_ref, accu_ref, accd_ref, gvacc_ref, act_ref, gup_ref, go_ref, sems_u, sems_d,
    ) = refs[n_all:]
    step = pl.program_id(0)
    last = pl.num_programs(0) - 1

    @pl.when(step == 0)
    def _():
        copies = load_pieces(place, refs[:n], metas_u, wu_ref, sems_u)
        copies += load_pieces(place, refs[n:n_all], metas_d, wd_ref, sems_d)
        accu_ref[...] = jnp.zeros_like(accu_ref)
        accd_ref[...] = jnp.zeros_like(accd_ref)
        gvacc_ref[...] = jnp.zeros_like(gvacc_ref)
        wait_all(copies)

    hidden = hidden_ref[...]
    n, rstd = norm_parts(hidden)
    normed = (n * vec_ref[2:3] + vec_ref[3:4]).astype(BF)
    row = lax.broadcasted_iota(jnp.int32, (ROWS, 1), 0) + step * ROWS
    go = jnp.where(row < live[0] * SEQ, cot_ref[...].astype(F32), 0.0)
    go_ref[...] = go.astype(BF)
    for m in range(HALVES):
        cols = slice(m * FW, (m + 1) * FW)
        up = nn(normed, wu_ref[m * D : (m + 1) * D])
        ga = nn(go_ref[...], wd_ref[m * D : (m + 1) * D])
        sq = up * up
        th = jnp.tanh(up * (GELU_A + (GELU_A * GELU_B) * sq))
        half = 0.5 + 0.5 * th
        act_ref[:, cols] = (up * half).astype(BF)
        slope = half + (0.5 * up) * (1.0 - th * th) * (GELU_A + (3.0 * GELU_A * GELU_B) * sq)
        gup_ref[:, cols] = (ga * slope).astype(BF)
    down = jnp.zeros((ROWS, D), F32)
    gy = jnp.zeros((ROWS, D), F32)
    for m in range(HALVES):
        cols = slice(m * FW, (m + 1) * FW)
        down += nt(act_ref[:, cols], wd_ref[m * D : (m + 1) * D])
        gy += nt(gup_ref[:, cols], wu_ref[m * D : (m + 1) * D])
        accu_ref[m] += tn(normed, gup_ref[:, cols])
        accd_ref[m] += tn(go_ref[...], act_ref[:, cols])
    mixed_ref[...] = (hidden + down).astype(BF)
    gh_ref[...] = go + norm_back(n, rstd, vec_ref[2:3], gy)
    gvacc_ref[0] += fold_rows(gy * n)
    gvacc_ref[1] += fold_rows(gy)

    @pl.when(step == last)
    def _():
        store_blocks(place, accu_ref, 0, own_ref, other_ref)
        store_blocks(place, accd_ref, FW, own_ref, other_ref)
        gv_ref[0:1] = jnp.sum(gvacc_ref[0], axis=0, keepdims=True)
        gv_ref[1:2] = jnp.sum(gvacc_ref[1], axis=0, keepdims=True)


def attn_backward_kernel(
    place, metas_qk, metas_vo, x_ref, gh_ref, q_ref, k_ref, v_ref, p_ref, ho_ref, vec_ref, gvtwo_ref, *refs
):
    n, n_all = len(metas_qk), len(metas_qk) + len(metas_vo)
    (
        gi_ref, own_ref, other_ref,
        wqk_ref, wvo_ref, acc_ref, gvacc_ref, gvec_ref, s_ref, ds_ref, dh_ref, dqkv_ref, sems_qk, sems_vo,
    ) = refs[n_all:]
    step = pl.program_id(0)
    last = pl.num_programs(0) - 1

    @pl.when(step == 0)
    def _():
        copies = load_pieces(place, refs[:n], metas_qk, wqk_ref, sems_qk)
        copies += load_pieces(place, refs[n:n_all], metas_vo, wvo_ref, sems_vo)
        acc_ref[...] = jnp.zeros_like(acc_ref)
        gvacc_ref[...] = jnp.zeros_like(gvacc_ref)
        wait_all(copies)

    x = x_ref[...].astype(F32)
    n, rstd = norm_parts(x)
    normed = (n * vec_ref[0:1] + vec_ref[1:2]).astype(BF)
    gh = gh_ref[...]
    gat = gh.astype(BF)
    for m in range(HALVES):
        cols = slice(m * HW, (m + 1) * HW)
        wo = slice(3 * HW, 4 * HW)
        dh_ref[:, cols] = nn(gat, wvo_ref[m * D : (m + 1) * D, HW:]).astype(BF)
        acc_ref[m, :, wo] += tn(gat, ho_ref[:, cols])
    for s in range(SEQS_STEP):
        for m in range(HALVES):
            at = seq_slice(s, m, HW)
            s_ref[at] = nt(v_ref[at], per_head(dh_ref[at]))
    for s in range(SEQS_STEP):
        for c in range(D // (2 * HEAD)):
            at = seq_slice(s, c, 2 * HEAD)
            probs = p_ref[at].astype(F32)
            gp = s_ref[at]
            delta = jnp.sum(probs * gp, axis=0, keepdims=True)
            ds_ref[at] = (probs * ((gp - delta) * HEAD**-0.5)).astype(BF)
    for s in range(SEQS_STEP):
        for m in range(HALVES):
            at = seq_slice(s, m, HW)
            rows = at[0]
            base = 3 * HW * m
            dqkv_ref[rows, base + 2 * HW : base + 3 * HW] = nn(p_ref[at], per_head(dh_ref[at])).astype(BF)
            dqkv_ref[rows, base + HW : base + 2 * HW] = nn(ds_ref[at], per_head(q_ref[at])).astype(BF)
    for s in range(SEQS_STEP):
        for c in range(D // (2 * HEAD)):
            at = seq_slice(s, c, 2 * HEAD)
            base = 3 * HW * (c // 2) + 2 * HEAD * (c % 2)
            dqkv_ref[at[0], base : base + 2 * HEAD] = pair_blocks(tn(ds_ref[at], k_ref[at])).astype(BF)
    gy = jnp.zeros((ROWS, D), F32)
    for m in range(HALVES):
        cols = slice(3 * HW * m, 3 * HW * (m + 1))
        gy += nt(dqkv_ref[:, cols.start : cols.start + 2 * HW], wqk_ref[m * D : (m + 1) * D, : 2 * HW])
        gy += nt(dqkv_ref[:, cols.start + 2 * HW : cols.stop], wvo_ref[m * D : (m + 1) * D, :HW])
        acc_ref[m, :, : 3 * HW] += tn(normed, dqkv_ref[:, cols])
    gi_ref[...] = gh + norm_back(n, rstd, vec_ref[0:1], gy)
    gvacc_ref[0] += fold_rows(gy * n)
    gvacc_ref[1] += fold_rows(gy)

    @pl.when(step == last)
    def _():
        store_blocks(place, acc_ref, 0, own_ref, other_ref)
        one = jnp.concatenate([jnp.sum(gvacc_ref[i], axis=0, keepdims=True) for i in range(2)], axis=0)
        rows = jnp.concatenate([one, gvtwo_ref[...], jnp.zeros((GC - 4, D), F32)], axis=0)
        for m in range(HALVES):
            gvec_ref[m] = rows.T
        store_blocks(place, gvec_ref, 4 * HW, own_ref, other_ref)


def row_block(width):
    return pl.BlockSpec((ROWS, width), lambda i, *_: (i, 0))


def held(shape):
    return pl.BlockSpec(shape, lambda i, *_: (0,) * len(shape), pipeline_mode=pl.Buffered(1))


def shape(dims, dtype):
    return jax.ShapeDtypeStruct(dims, dtype)


PARAMS = pltpu.CompilerParams(vmem_limit_bytes=56 * 1024 * 1024)
HBM = pl.BlockSpec(memory_space=pl.ANY)


def weight_scratch(pieces, metas):
    copies = sum(len(meta) for meta in metas)
    return pltpu.VMEM((HALVES * D, pieces[0].shape[1]), BF), pltpu.SemaphoreType.DMA((copies,))


def cost(flops, nbytes):
    return pl.CostEstimate(flops=flops, bytes_accessed=nbytes, transcendentals=0)


def attn_scores(place, frames, tokens, group):
    rows = tokens.shape[0]
    pieces, metas = group
    w, sems = weight_scratch(pieces, metas)
    return pl.pallas_call(
        lambda place, frames, *refs: attn_scores_kernel(place, frames, metas, *refs),
        grid_spec=pltpu.PrefetchScalarGridSpec(
            num_scalar_prefetch=2,
            grid=(rows // ROWS,),
            in_specs=[row_block(D)] + [HBM] * len(pieces),
            out_specs=[row_block(D)] * 4 + [held((8, D))],
            scratch_shapes=[w, pltpu.VMEM((ROWS, D), F32), sems],
        ),
        out_shape=[shape((rows, D), BF)] * 4 + [shape((8, D), F32)],
        compiler_params=PARAMS,
        cost_estimate=cost(rows * D * 2 * D * 2 * 2, rows * D * 10),
        name="attn_scores",
    )(place, frames, tokens, *pieces)


def attn_output(place, tokens, normed, p, group):
    rows = tokens.shape[0]
    pieces, metas = group
    w, sems = weight_scratch(pieces, metas)
    return pl.pallas_call(
        lambda place, *refs: attn_output_kernel(place, metas, *refs),
        grid_spec=pltpu.PrefetchScalarGridSpec(
            num_scalar_prefetch=1,
            grid=(rows // ROWS,),
            in_specs=[row_block(D)] * 3 + [HBM] * len(pieces),
            out_specs=[row_block(D)] * 3,
            scratch_shapes=[w, sems],
        ),
        out_shape=[shape((rows, D), BF)] * 2 + [shape((rows, D), F32)],
        compiler_params=PARAMS,
        cost_estimate=cost(rows * D * 2 * D * 2 * 2, rows * D * 14),
        name="attn_output",
    )(place, tokens, normed, p, *pieces)


def feed_forward(place, live, hidden, cotangent, vec, up, down, out_dims):
    rows = hidden.shape[0]
    wu, sems_u = weight_scratch(*up)
    wd, sems_d = weight_scratch(*down)
    grads = out_dims + (2 * FW,)
    return pl.pallas_call(
        lambda place, live, *refs: feed_forward_kernel(place, live, up[1], down[1], *refs),
        grid_spec=pltpu.PrefetchScalarGridSpec(
            num_scalar_prefetch=2,
            grid=(rows // ROWS,),
            in_specs=[row_block(D), row_block(D), held((8, D))] + [HBM] * (len(up[0]) + len(down[0])),
            out_specs=[row_block(D), row_block(D), held(grads), held(grads), held((2, D))],
            scratch_shapes=[
                wu,
                wd,
                pltpu.VMEM((HALVES, D, FW), F32),
                pltpu.VMEM((HALVES, D, FW), F32),
                pltpu.VMEM((2, 8, D), F32),
                pltpu.VMEM((ROWS, FF), BF),
                pltpu.VMEM((ROWS, FF), BF),
                pltpu.VMEM((ROWS, D), BF),
                sems_u,
                sems_d,
            ],
        ),
        out_shape=[
            shape((rows, D), BF),
            shape((rows, D), F32),
            shape(grads, BF),
            shape(grads, BF),
            shape((2, D), F32),
        ],
        compiler_params=PARAMS,
        cost_estimate=cost(rows * D * FF * 12, rows * D * 12),
        name="feed_forward",
    )(place, live, hidden, cotangent, vec, *up[0], *down[0])


def attn_backward(place, tokens, gh, q, k, v, p, ho, vec, gv_two, qk, vo, out_dims):
    rows = tokens.shape[0]
    wqk, sems_qk = weight_scratch(*qk)
    wvo, sems_vo = weight_scratch(*vo)
    grads = out_dims + (4 * HW + GC,)
    return pl.pallas_call(
        lambda place, *refs: attn_backward_kernel(place, qk[1], vo[1], *refs),
        grid_spec=pltpu.PrefetchScalarGridSpec(
            num_scalar_prefetch=1,
            grid=(rows // ROWS,),
            in_specs=[row_block(D)] * 7 + [held((8, D)), held((2, D))] + [HBM] * (len(qk[0]) + len(vo[0])),
            out_specs=[row_block(D), held(grads), held(grads)],
            scratch_shapes=[
                wqk,
                wvo,
                pltpu.VMEM((HALVES, D, 4 * HW), F32),
                pltpu.VMEM((2, 8, D), F32),
                pltpu.VMEM((HALVES, D, GC), F32),
                pltpu.VMEM((ROWS, D), F32),
                pltpu.VMEM((ROWS, D), BF),
                pltpu.VMEM((ROWS, D), BF),
                pltpu.VMEM((ROWS, 3 * D), BF),
                sems_qk,
                sems_vo,
            ],
        ),
        out_shape=[shape((rows, D), F32), shape(grads, BF), shape(grads, BF)],
        compiler_params=PARAMS,
        cost_estimate=cost(rows * D * 4 * D * 8, rows * D * 20),
        name="attn_backward",
    )(place, tokens, gh, q, k, v, p, ho, vec, gv_two, *qk[0], *vo[0])


def build(mesh):
    n_dp, n_mp = mesh.shape["dp"], mesh.shape["mp"]
    n_z = n_dp // 4
    depth = D // n_dp
    staged = n_mp == HALVES
    both = ("dp", "mp")
    PLANE = ((0, 0), (1, 0), (0, 1), (1, 1))

    def send(value, zr=0, xr=0, yr=0, cr=0):
        pairs = []
        for z in range(n_z):
            for x in range(2):
                for c in range(2):
                    for y in range(n_mp):
                        here = ((z * 2 + x) * 2 + c) * n_mp + y
                        there = ((((z + zr) % n_z) * 2 + (x ^ xr)) * 2 + (c ^ cr)) * n_mp + (y ^ yr)
                        pairs.append((here, there))
        return lax.ppermute(value, both, pairs)

    def along_z(value):
        return [value] + [send(value, zr=r) for r in range(1, n_z)]

    def across_plane(value):
        return [value] + [send(value, xr=x, yr=y) for x, y in PLANE[1:]]

    def both_cores(pieces):
        return pieces + [send(piece, cr=1) for piece in pieces]

    def stack(blocks):
        return jnp.concatenate(blocks, axis=0)

    Z_FIRST = tuple(tuple((c, x, y, z) for z in range(n_z)) for c in range(2) for x, y in PLANE)
    PLANE_FIRST = tuple(tuple((c, x, y, z) for x, y in PLANE) for c in range(2) for z in range(n_z))

    def after(value, *others):
        return lax.optimization_barrier((value,) + others)[0]

    def gather_staged(qk, vo, up, down):
        down_plane = across_plane(down)
        qk_z = along_z(qk)
        vo_z = along_z(after(vo, qk_z[-1]))
        qk_plane = across_plane(stack(qk_z))
        qk_all = both_cores(qk_plane)
        up_z = along_z(after(up, vo_z[-1]))
        vo_all = both_cores(across_plane(after(stack(vo_z), qk_plane[-1])))
        down_all = both_cores(along_z(after(stack(down_plane), up_z[-1])))
        up_all = both_cores(across_plane(after(stack(up_z), vo_all[3])))
        return (qk_all, Z_FIRST), (vo_all, Z_FIRST), (up_all, Z_FIRST), (down_all, PLANE_FIRST)

    def gather_plain(block, parts):
        out = lax.all_gather(block, ("mp", "dp"), axis=0, tiled=True)
        out = out.reshape(HALVES, n_mp // HALVES, D, parts, -1)
        return out.transpose(0, 2, 3, 1, 4).reshape(HALVES * D, -1)

    def plain_pieces(whole):
        z, x, c = lax.axis_index("dp") // 4, (lax.axis_index("dp") // 2) % 2, lax.axis_index("dp") % 2
        y = lax.axis_index("mp") % HALVES
        blocks = whole.reshape(HALVES, n_z, 2, 2, depth, -1)
        index = lambda n, at: (at - jnp.arange(n)) % n
        blocks = blocks[:, index(n_z, z)]
        blocks = blocks[y ^ jnp.arange(2)][:, :, x ^ jnp.arange(2)][:, :, :, c ^ jnp.arange(2)]
        blocks = blocks.transpose(3, 0, 2, 1, 4, 5).reshape(8, n_z * depth, -1)
        return [blocks[i] for i in range(8)], Z_FIRST

    def scatter_staged(own, other):
        mine = own.astype(F32) + send(other, cr=1).astype(F32)
        mine = mine.astype(BF)
        got = [send(mine[x + 2 * y], xr=x, yr=y).astype(F32) for x, y in PLANE[1:]]
        mine = ((mine[0].astype(F32) + got[0]) + (got[1] + got[2])).astype(BF)
        total = mine[0].astype(F32)
        for r in range(1, n_z):
            total += send(mine[r], zr=r).astype(F32)
        return total

    def scatter_plain(own, other, parts):
        z, x, c = lax.axis_index("dp") // 4, (lax.axis_index("dp") // 2) % 2, lax.axis_index("dp") % 2
        y = lax.axis_index("mp") % HALVES
        blocks = jnp.stack([own, other]).reshape(2, 2, 2, n_z, depth, -1)
        blocks = blocks[c ^ jnp.arange(2)][:, y ^ jnp.arange(2)][:, :, x ^ jnp.arange(2)]
        blocks = blocks[:, :, :, (jnp.arange(n_z) - z) % n_z]
        blocks = blocks.transpose(1, 3, 2, 0, 4, 5).reshape(HALVES, D, -1)
        wide = sum(parts)
        main, tail = blocks[:, :, :wide], blocks[:, :, wide:]
        main = main.reshape(HALVES, D, len(parts), n_mp // HALVES, -1).transpose(0, 3, 1, 2, 4)
        main = main.reshape(n_mp, D, -1)
        tail = jnp.broadcast_to(tail[:1], (n_mp, D, tail.shape[2]))
        flat = jnp.concatenate([main, tail], axis=2).reshape(n_mp * D, -1)
        return lax.psum_scatter(flat, ("mp", "dp"), scatter_dimension=0, tiled=True).astype(F32)

    def shards(
        tokens, cotangent, frame_count, live_count, w_query, w_key, w_value, w_out, w_up, w_down,
        gain_one, shift_one, gain_two, shift_two,
    ):
        dp, mp = lax.axis_index("dp"), lax.axis_index("mp")
        place = jnp.stack([dp // 4, (dp // 2) % 2, dp % 2, mp % HALVES, jnp.int32(n_z)]).astype(jnp.int32)
        seqs = tokens.shape[0] // SEQ
        frames = lax.dynamic_slice(frame_count, (mp * seqs,), (seqs,))
        live = live_count - mp * seqs
        vec = jnp.stack([gain_one, shift_one, gain_two, shift_two], axis=1)
        vec = jnp.pad(vec, ((0, 0), (0, GC - 4)))
        if staged:
            qk, vo, up, down = gather_staged(
                jnp.concatenate([w_query, w_key, vec], axis=1),
                jnp.concatenate([w_value, w_out.T], axis=1),
                w_up,
                w_down.T,
            )
        else:
            vec = lax.all_gather(vec, "dp", axis=0, tiled=True)
            whole = gather_plain(jnp.concatenate([w_query, w_key], axis=1), 2)
            qk = plain_pieces(jnp.concatenate([whole, jnp.concatenate([vec] * HALVES)], axis=1))
            vo = plain_pieces(gather_plain(jnp.concatenate([w_value, w_out.T], axis=1), 2))
            up = plain_pieces(gather_plain(w_up, 1))
            down = plain_pieces(gather_plain(w_down.T, 1))
        out_dims = (4, n_z, depth)
        normed, q, k, p, vec = attn_scores(place, frames, tokens, qk)
        v, ho, hidden = attn_output(place, tokens, normed, p, vo)
        mixed, gh, f_own, f_other, gv_two = feed_forward(
            place, live, hidden, cotangent, vec, up, down, out_dims
        )
        grad_input, a_own, a_other = attn_backward(
            place, tokens, gh, q, k, v, p, ho, vec, gv_two, qk, vo, out_dims
        )
        if staged:
            gf = scatter_staged(f_own, f_other)
            ga = scatter_staged(a_own, a_other)
        else:
            gf = scatter_plain(f_own, f_other, (FW, FW))
            ga = scatter_plain(a_own, a_other, (HW,) * 4)
        wide = w_query.shape[1]
        tall = w_up.shape[1]
        gains = ga[:, 4 * wide :]
        return (
            mixed,
            grad_input,
            ga[:, :wide],
            ga[:, wide : 2 * wide],
            ga[:, 2 * wide : 3 * wide],
            ga[:, 3 * wide : 4 * wide].T,
            gf[:, :tall],
            gf[:, tall:].T,
            gains[:, 0],
            gains[:, 1],
            gains[:, 2],
            gains[:, 3],
        )

    return shards


def solution(mesh):
    rows = P(("dp", "mp"), None)
    wide, tall, dp = P("dp", "mp"), P("mp", "dp"), P("dp")
    return jax.shard_map(
        build(mesh),
        mesh=mesh,
        in_specs=(rows, rows, dp, dp, wide, wide, wide, tall, wide, tall, dp, dp, dp, dp),
        out_specs=(rows, rows, wide, wide, wide, tall, wide, tall, dp, dp, dp, dp),
        check_vma=False,
    )
```

```python
import jax
import jax.numpy as jnp
from jax import lax
from jax.experimental import pallas as pl
from jax.experimental.pallas import tpu as pltpu
from jax.sharding import PartitionSpec as P

D = 512
FF = 2048
HEAD = 64
FTOK = 8
SEQ = 48
HALVES = 2
HW = D // HALVES
FW = FF // HALVES
PAIR = 2 * HEAD
GC = 128
EPS = 1e-05
CHUNK = 256
BF = jnp.bfloat16
F32 = jnp.float32


def nn(a, b):
    return lax.dot_general(a, b, (((1,), (0,)), ((), ())), preferred_element_type=F32)


def nt(a, b):
    return lax.dot_general(a, b, (((1,), (1,)), ((), ())), preferred_element_type=F32)


def tn(a, b):
    return lax.dot_general(a, b, (((0,), (0,)), ((), ())), preferred_element_type=F32)


def norm_parts(rows):
    mean = jnp.mean(rows, axis=-1, keepdims=True)
    centered = rows - mean
    spread = jnp.mean(centered * centered, axis=-1, keepdims=True)
    rstd = lax.rsqrt(spread + EPS)
    return centered * rstd, rstd


def norm_back(n, rstd, gain, gy):
    gg = gy * gain
    first = jnp.mean(gg, axis=-1, keepdims=True)
    second = jnp.mean(gg * n, axis=-1, keepdims=True)
    return rstd * (gg - first - n * second)


def fold_rows(value):
    return jnp.sum(value.reshape(value.shape[0] // 8, 8, value.shape[1]), axis=0)


def per_head(rows):
    width = rows.shape[1]
    lane = lax.broadcasted_iota(jnp.int32, rows.shape, 1) // HEAD
    pad = jnp.zeros((HEAD - SEQ, width), rows.dtype)
    parts = []
    for h in range(width // HEAD):
        parts.append(jnp.where(lane == h, rows, jnp.zeros_like(rows)))
        parts.append(pad)
    return jnp.concatenate(parts, axis=0)


def pair_blocks(product):
    lane = lax.broadcasted_iota(jnp.int32, (SEQ, PAIR), 1)
    return jnp.where(lane < HEAD, product[:SEQ], product[HEAD : HEAD + SEQ])


def seq_slice(s, c, width):
    return (slice(s * SEQ, (s + 1) * SEQ), slice(c * width, (c + 1) * width))


def block_place(place, cr, xr, yr, zr):
    z, x, c, y = place[0], place[1], place[2], place[3]
    z = lax.rem(z - zr + place[4], place[4])
    return (y ^ yr, z * 4 + (x ^ xr) * 2 + (c ^ cr))


def load_pieces(place, pieces, metas, dst, sems):
    copies = []
    for piece, meta in zip(pieces, metas):
        depth = piece.shape[0] // len(meta)
        n_dp = D // depth
        for b, rel in enumerate(meta):
            m, dp = block_place(place, *rel)
            row = pl.multiple_of((m * n_dp + dp) * depth, depth)
            copy = pltpu.make_async_copy(
                piece.at[pl.ds(b * depth, depth), :], dst.at[pl.ds(row, depth), :], sems.at[len(copies)]
            )
            copy.start()
            copies.append(copy)
    return copies


def wait_all(copies):
    for copy in copies:
        copy.wait()


def store_blocks(place, acc, start, own_ref, other_ref):
    slots, n_z, depth, width = own_ref.shape
    n_dp = n_z * 4
    for core in range(2):

        @pl.when(place[2] == core)
        def _():
            for m in range(HALVES):
                for dp in range(n_dp):
                    z, x, c = dp // 4, (dp // 2) % 2, dp % 2
                    slot = (place[1] ^ x) + 2 * (place[3] ^ m)
                    back = lax.rem(z - place[0] + n_z, n_z)
                    rows = slice(dp * depth, (dp + 1) * depth)
                    ref = own_ref if c == core else other_ref
                    ref[slot, back, :, start : start + acc.shape[2]] = acc[m, rows, :].astype(BF)


def attn_forward_kernel(place, frames, metas, x_ref, *refs):
    n = len(metas)
    pieces = refs[:n]
    q_ref, k_ref, v_ref, p_ref, ho_ref, hidden_ref, vec_ref, w_ref, s_ref, sems = refs[n:]
    step = pl.program_id(0)
    seqs = x_ref.shape[0] // SEQ

    @pl.when(step == 0)
    def _():
        wait_all(load_pieces(place, pieces, metas, w_ref, sems))
        vec_ref[...] = w_ref[:D, 4 * HW :].astype(F32).T[:8]

    x = x_ref[...].astype(F32)
    n, _ = norm_parts(x)
    normed = (n * vec_ref[0:1] + vec_ref[1:2]).astype(BF)
    for m in range(HALVES):
        qkv = nn(normed, w_ref[m * D : (m + 1) * D, : 3 * HW]).astype(BF)
        cols = slice(m * HW, (m + 1) * HW)
        q_ref[:, cols] = qkv[:, :HW]
        k_ref[:, cols] = qkv[:, HW : 2 * HW]
        v_ref[:, cols] = qkv[:, 2 * HW :]
    for s in range(seqs):
        for m in range(HALVES):
            at = seq_slice(s, m, HW)
            s_ref[at] = nt(k_ref[at], per_head(q_ref[at]))
    key = lax.broadcasted_iota(jnp.int32, (SEQ, PAIR), 0)
    query = lax.broadcasted_iota(jnp.int32, (SEQ, PAIR), 1) % HEAD
    for s in range(seqs):
        allowed = (key <= query) & (key < frames[step * seqs + s] * FTOK)
        for c in range(D // PAIR):
            at = seq_slice(s, c, PAIR)
            scores = jnp.where(allowed, s_ref[at] * HEAD**-0.5, -1000000000.0)
            expd = jnp.exp(scores - jnp.max(scores, axis=0, keepdims=True))
            p_ref[at] = (expd * (1.0 / jnp.sum(expd, axis=0, keepdims=True))).astype(BF)
    for s in range(seqs):
        for c in range(D // PAIR):
            at = seq_slice(s, c, PAIR)
            ho_ref[at] = pair_blocks(tn(p_ref[at], v_ref[at])).astype(BF)
    attended = nt(ho_ref[:, :HW], w_ref[:D, 3 * HW : 4 * HW]) + nt(ho_ref[:, HW:], w_ref[D:, 3 * HW : 4 * HW])
    hidden_ref[...] = x + attended


GELU_A = (2.0 / jnp.pi) ** 0.5
GELU_B = 0.044715


def feed_forward_kernel(place, live, metas, hidden_ref, cot_ref, ho_ref, vec_ref, *refs):
    n = len(metas)
    (
        mixed_ref, gh_ref, own_ref, other_ref, gv_ref,
        w_ref, accu_ref, accd_ref, acco_ref, gvacc_ref, act_ref, gup_ref, go_ref, sems,
    ) = refs[n:]
    step = pl.program_id(0)
    last = pl.num_programs(0) - 1
    rows = hidden_ref.shape[0]

    @pl.when(step == 0)
    def _():
        copies = load_pieces(place, refs[:n], metas, w_ref, sems)
        accu_ref[...] = jnp.zeros_like(accu_ref)
        accd_ref[...] = jnp.zeros_like(accd_ref)
        acco_ref[...] = jnp.zeros_like(acco_ref)
        gvacc_ref[...] = jnp.zeros_like(gvacc_ref)
        wait_all(copies)

    hidden = hidden_ref[...]
    n, rstd = norm_parts(hidden)
    normed = (n * vec_ref[2:3] + vec_ref[3:4]).astype(BF)
    row = lax.broadcasted_iota(jnp.int32, (rows, 1), 0) + step * rows
    go = jnp.where(row < live[0] * SEQ, cot_ref[...].astype(F32), 0.0)
    go_ref[...] = go.astype(BF)
    for m in range(HALVES):
        for c in range(FW // CHUNK):
            depth = slice(m * D, (m + 1) * D)
            cols = slice(m * FW + c * CHUNK, m * FW + (c + 1) * CHUNK)
            up = nn(normed, w_ref[depth, c * CHUNK : (c + 1) * CHUNK])
            ga = nn(go_ref[...], w_ref[depth, FW + c * CHUNK : FW + (c + 1) * CHUNK])
            sq = up * up
            th = jnp.tanh(up * (GELU_A + (GELU_A * GELU_B) * sq))
            half = 0.5 + 0.5 * th
            act_ref[:, cols] = (up * half).astype(BF)
            slope = half + (0.5 * up) * (1.0 - th * th) * (GELU_A + (3.0 * GELU_A * GELU_B) * sq)
            gup_ref[:, cols] = (ga * slope).astype(BF)
    down = jnp.zeros((rows, D), F32)
    gy = jnp.zeros((rows, D), F32)
    for m in range(HALVES):
        cols = slice(m * FW, (m + 1) * FW)
        down += nt(act_ref[:, cols], w_ref[m * D : (m + 1) * D, FW:])
        gy += nt(gup_ref[:, cols], w_ref[m * D : (m + 1) * D, :FW])
        accu_ref[m] += tn(normed, gup_ref[:, cols])
        accd_ref[m] += tn(go_ref[...], act_ref[:, cols])
    mixed_ref[...] = (hidden + down).astype(BF)
    gh = go + norm_back(n, rstd, vec_ref[2:3], gy)
    gh_ref[...] = gh
    for m in range(HALVES):
        acco_ref[m] += tn(gh.astype(BF), ho_ref[:, m * HW : (m + 1) * HW])
    gvacc_ref[0] += fold_rows(gy * n)
    gvacc_ref[1] += fold_rows(gy)

    @pl.when(step == last)
    def _():
        store_blocks(place, accu_ref, 0, own_ref, other_ref)
        store_blocks(place, accd_ref, FW, own_ref, other_ref)
        store_blocks(place, acco_ref, 2 * FW, own_ref, other_ref)
        gv_ref[0:1] = jnp.sum(gvacc_ref[0], axis=0, keepdims=True)
        gv_ref[1:2] = jnp.sum(gvacc_ref[1], axis=0, keepdims=True)


def attn_backward_kernel(
    place, x_ref, gh_ref, q_ref, k_ref, v_ref, p_ref, w_ref, vec_ref, gvtwo_ref,
    gi_ref, own_ref, other_ref, acc_ref, gvacc_ref, gvec_ref, s_ref, ds_ref, dh_ref, dqkv_ref,
):
    step = pl.program_id(0)
    last = pl.num_programs(0) - 1
    seqs = x_ref.shape[0] // SEQ

    @pl.when(step == 0)
    def _():
        acc_ref[...] = jnp.zeros_like(acc_ref)
        gvacc_ref[...] = jnp.zeros_like(gvacc_ref)

    gh = gh_ref[...]
    gat = gh.astype(BF)
    for m in range(HALVES):
        dh_ref[:, m * HW : (m + 1) * HW] = nn(gat, w_ref[m * D : (m + 1) * D, 3 * HW : 4 * HW]).astype(BF)
    for s in range(seqs):
        for c in range(D // PAIR):
            at = seq_slice(s, c, PAIR)
            s_ref[at] = nt(v_ref[at], per_head(dh_ref[at]))
    for s in range(seqs):
        for c in range(D // PAIR):
            at = seq_slice(s, c, PAIR)
            probs = p_ref[at].astype(F32)
            gp = s_ref[at]
            delta = jnp.sum(probs * gp, axis=0, keepdims=True)
            ds_ref[at] = (probs * ((gp - delta) * HEAD**-0.5)).astype(BF)
    for s in range(seqs):
        for c in range(D // PAIR):
            at = seq_slice(s, c, PAIR)
            base = 3 * HW * (c * PAIR // HW) + c * PAIR % HW
            dqkv_ref[at[0], base + 2 * HW : base + 2 * HW + PAIR] = nn(p_ref[at], per_head(dh_ref[at])).astype(BF)
            dqkv_ref[at[0], base + HW : base + HW + PAIR] = nn(ds_ref[at], per_head(q_ref[at])).astype(BF)
    for s in range(seqs):
        for c in range(D // PAIR):
            at = seq_slice(s, c, PAIR)
            base = 3 * HW * (c * PAIR // HW) + c * PAIR % HW
            dqkv_ref[at[0], base : base + PAIR] = pair_blocks(tn(ds_ref[at], k_ref[at])).astype(BF)
    n, rstd = norm_parts(x_ref[...].astype(F32))
    normed = (n * vec_ref[0:1] + vec_ref[1:2]).astype(BF)
    gy = jnp.zeros(x_ref.shape, F32)
    for m in range(HALVES):
        cols = slice(3 * HW * m, 3 * HW * (m + 1))
        gy += nt(dqkv_ref[:, cols], w_ref[m * D : (m + 1) * D, : 3 * HW])
        acc_ref[m] += tn(normed, dqkv_ref[:, cols])
    gi_ref[...] = gh + norm_back(n, rstd, vec_ref[0:1], gy)
    gvacc_ref[0] += fold_rows(gy * n)
    gvacc_ref[1] += fold_rows(gy)

    @pl.when(step == last)
    def _():
        store_blocks(place, acc_ref, 0, own_ref, other_ref)
        one = jnp.concatenate([jnp.sum(gvacc_ref[i], axis=0, keepdims=True) for i in range(2)], axis=0)
        rows = jnp.concatenate([one, gvtwo_ref[...], jnp.zeros((GC - 4, D), F32)], axis=0)
        for m in range(HALVES):
            gvec_ref[m] = rows.T
        store_blocks(place, gvec_ref, 3 * HW, own_ref, other_ref)


def step_rows(rows):
    return 16 * SEQ if rows % (16 * SEQ) == 0 else 8 * SEQ


def row_block(rows, width):
    return pl.BlockSpec((step_rows(rows), width), lambda i, *_: (i, 0))


def held(shape):
    return pl.BlockSpec(shape, lambda i, *_: (0,) * len(shape), pipeline_mode=pl.Buffered(1))


def shape(dims, dtype):
    return jax.ShapeDtypeStruct(dims, dtype)


PARAMS = pltpu.CompilerParams(vmem_limit_bytes=60 * 1024 * 1024)
HBM = pl.BlockSpec(memory_space=pl.ANY)


def weight_dims(group):
    return (HALVES * D, group[0][0].shape[1])


def copy_sems(group):
    return pltpu.SemaphoreType.DMA((sum(len(meta) for meta in group[1]),))


def cost(flops, nbytes):
    return pl.CostEstimate(flops=flops, bytes_accessed=nbytes, transcendentals=0)


def attn_forward(place, frames, tokens, group):
    rows = tokens.shape[0]
    dims = weight_dims(group)
    return pl.pallas_call(
        lambda place, frames, *refs: attn_forward_kernel(place, frames, group[1], *refs),
        grid_spec=pltpu.PrefetchScalarGridSpec(
            num_scalar_prefetch=2,
            grid=(rows // step_rows(rows),),
            in_specs=[row_block(rows, D)] + [HBM] * len(group[0]),
            out_specs=[row_block(rows, D)] * 6 + [held((8, D)), held(dims)],
            scratch_shapes=[pltpu.VMEM((step_rows(rows), D), F32), copy_sems(group)],
        ),
        out_shape=[shape((rows, D), BF)] * 5 + [shape((rows, D), F32), shape((8, D), F32), shape(dims, BF)],
        compiler_params=PARAMS,
        cost_estimate=cost(rows * D * D * 24, rows * D * 18),
        name="attn_forward",
    )(place, frames, tokens, *group[0])


def feed_forward(place, live, hidden, cotangent, ho, vec, group, out_dims):
    rows = hidden.shape[0]
    grads = out_dims + (2 * FW + HW,)
    dims = weight_dims(group)
    return pl.pallas_call(
        lambda place, live, *refs: feed_forward_kernel(place, live, group[1], *refs),
        grid_spec=pltpu.PrefetchScalarGridSpec(
            num_scalar_prefetch=2,
            grid=(rows // step_rows(rows),),
            in_specs=[row_block(rows, D)] * 3 + [held((8, D))] + [HBM] * len(group[0]),
            out_specs=[row_block(rows, D), row_block(rows, D), held(grads), held(grads), held((2, D))],
            scratch_shapes=[
                pltpu.VMEM(dims, BF),
                pltpu.VMEM((HALVES, D, FW), F32),
                pltpu.VMEM((HALVES, D, FW), F32),
                pltpu.VMEM((HALVES, D, HW), F32),
                pltpu.VMEM((2, 8, D), F32),
                pltpu.VMEM((step_rows(rows), FF), BF),
                pltpu.VMEM((step_rows(rows), FF), BF),
                pltpu.VMEM((step_rows(rows), D), BF),
                copy_sems(group),
            ],
        ),
        out_shape=[
            shape((rows, D), BF),
            shape((rows, D), F32),
            shape(grads, BF),
            shape(grads, BF),
            shape((2, D), F32),
        ],
        compiler_params=PARAMS,
        cost_estimate=cost(rows * D * FF * 12, rows * D * 12),
        name="feed_forward",
    )(place, live, hidden, cotangent, ho, vec, *group[0])


def attn_backward(place, tokens, gh, q, k, v, p, w, vec, gv_two, out_dims):
    rows = tokens.shape[0]
    grads = out_dims + (3 * HW + GC,)
    return pl.pallas_call(
        attn_backward_kernel,
        grid_spec=pltpu.PrefetchScalarGridSpec(
            num_scalar_prefetch=1,
            grid=(rows // step_rows(rows),),
            in_specs=[row_block(rows, D)] * 6 + [held(w.shape), held((8, D)), held((2, D))],
            out_specs=[row_block(rows, D), held(grads), held(grads)],
            scratch_shapes=[
                pltpu.VMEM((HALVES, D, 3 * HW), F32),
                pltpu.VMEM((2, 8, D), F32),
                pltpu.VMEM((HALVES, D, GC), F32),
                pltpu.VMEM((step_rows(rows), D), F32),
                pltpu.VMEM((step_rows(rows), D), BF),
                pltpu.VMEM((step_rows(rows), D), BF),
                pltpu.VMEM((step_rows(rows), 3 * D), BF),
            ],
        ),
        out_shape=[shape((rows, D), F32), shape(grads, BF), shape(grads, BF)],
        compiler_params=PARAMS,
        cost_estimate=cost(rows * D * D * 36, rows * D * 18),
        name="attn_backward",
    )(place, tokens, gh, q, k, v, p, w, vec, gv_two)


def build(mesh):
    n_dp, n_mp = mesh.shape["dp"], mesh.shape["mp"]
    n_z = n_dp // 4
    depth = D // n_dp
    staged = n_mp == HALVES
    both = ("dp", "mp")
    PLANE = ((0, 0), (1, 0), (0, 1), (1, 1))

    def send(value, zr=0, xr=0, yr=0, cr=0):
        pairs = []
        for z in range(n_z):
            for x in range(2):
                for c in range(2):
                    for y in range(n_mp):
                        here = ((z * 2 + x) * 2 + c) * n_mp + y
                        there = ((((z + zr) % n_z) * 2 + (x ^ xr)) * 2 + (c ^ cr)) * n_mp + (y ^ yr)
                        pairs.append((here, there))
        return lax.ppermute(value, both, pairs)

    def along_z(value):
        return [value] + [send(value, zr=r) for r in range(1, n_z)]

    def across_plane(value):
        return [value] + [send(value, xr=x, yr=y) for x, y in PLANE[1:]]

    def both_cores(pieces):
        return pieces + [send(piece, cr=1) for piece in pieces]

    def stack(blocks):
        return jnp.concatenate(blocks, axis=0)

    Z_FIRST = tuple(tuple((c, x, y, z) for z in range(n_z)) for c in range(2) for x, y in PLANE)
    PLANE_FIRST = tuple(tuple((c, x, y, z) for x, y in PLANE) for c in range(2) for z in range(n_z))

    def after(value, *others):
        return lax.optimization_barrier((value,) + others)[0]

    def gather_first(attn, ff):
        attn_z = along_z(attn)
        attn_plane = across_plane(stack(attn_z))
        ff_z = along_z(after(ff, attn_z[-1]))
        ff_plane = across_plane(after(stack(ff_z), attn_plane[-1]))
        return (both_cores(attn_plane), Z_FIRST), ff_plane

    def gather_last(ff_plane, done):
        ff_plane = [after(piece, done) for piece in ff_plane]
        return both_cores(ff_plane), Z_FIRST

    def gather_plain(block, parts):
        out = lax.all_gather(block, ("mp", "dp"), axis=0, tiled=True)
        out = out.reshape(HALVES, n_mp // HALVES, D, parts, -1)
        return out.transpose(0, 2, 3, 1, 4).reshape(HALVES * D, -1)

    def plain_pieces(whole):
        z, x, c = lax.axis_index("dp") // 4, (lax.axis_index("dp") // 2) % 2, lax.axis_index("dp") % 2
        y = lax.axis_index("mp") % HALVES
        blocks = whole.reshape(HALVES, n_z, 2, 2, depth, -1)
        index = lambda n, at: (at - jnp.arange(n)) % n
        blocks = blocks[:, index(n_z, z)]
        blocks = blocks[y ^ jnp.arange(2)][:, :, x ^ jnp.arange(2)][:, :, :, c ^ jnp.arange(2)]
        blocks = blocks.transpose(3, 0, 2, 1, 4, 5).reshape(8, n_z * depth, -1)
        return [blocks[i] for i in range(8)], Z_FIRST

    def scatter_core(own, other):
        return (own.astype(F32) + send(other, cr=1).astype(F32)).astype(BF)

    def scatter_plane(mine):
        return mine[0], [send(mine[x + 2 * y], xr=x, yr=y) for x, y in PLANE[1:]]

    def scatter_add(mine, got):
        got = [part.astype(F32) for part in got]
        return ((mine.astype(F32) + got[0]) + (got[1] + got[2])).astype(BF)

    def scatter_z(mine):
        return mine[0], [send(mine[r], zr=r) for r in range(1, n_z)]

    def scatter_sum(mine, got):
        total = mine.astype(F32)
        for part in got:
            total += part.astype(F32)
        return total

    def scatter_plain(own, other, parts):
        z, x, c = lax.axis_index("dp") // 4, (lax.axis_index("dp") // 2) % 2, lax.axis_index("dp") % 2
        y = lax.axis_index("mp") % HALVES
        blocks = jnp.stack([own, other]).reshape(2, 2, 2, n_z, depth, -1)
        blocks = blocks[c ^ jnp.arange(2)][:, y ^ jnp.arange(2)][:, :, x ^ jnp.arange(2)]
        blocks = blocks[:, :, :, (jnp.arange(n_z) - z) % n_z]
        blocks = blocks.transpose(1, 3, 2, 0, 4, 5).reshape(HALVES, D, -1)
        main, start = [], 0
        for part in parts:
            cut = blocks[:, :, start : start + part].reshape(HALVES, D, n_mp // HALVES, -1)
            main.append(cut.transpose(0, 2, 1, 3).reshape(n_mp, D, -1))
            start += part
        main = jnp.concatenate(main, axis=2)
        tail = jnp.broadcast_to(blocks[:1, :, start:], (n_mp, D, blocks.shape[2] - start))
        flat = jnp.concatenate([main, tail], axis=2).reshape(n_mp * D, -1)
        return lax.psum_scatter(flat, ("mp", "dp"), scatter_dimension=0, tiled=True).astype(F32)

    def shards(
        tokens, cotangent, frame_count, live_count, w_query, w_key, w_value, w_out, w_up, w_down,
        gain_one, shift_one, gain_two, shift_two,
    ):
        dp, mp = lax.axis_index("dp"), lax.axis_index("mp")
        place = jnp.stack([dp // 4, (dp // 2) % 2, dp % 2, mp % HALVES, jnp.int32(n_z)]).astype(jnp.int32)
        seqs = tokens.shape[0] // SEQ
        frames = lax.dynamic_slice(frame_count, (mp * seqs,), (seqs,))
        live = live_count - mp * seqs
        vec = jnp.stack([gain_one, shift_one, gain_two, shift_two], axis=1)
        vec = jnp.pad(vec, ((0, 0), (0, GC - 4)))
        attn = jnp.concatenate([w_query, w_key, w_value, w_out.T], axis=1)
        ff = jnp.concatenate([w_up, w_down.T], axis=1)
        out_dims = (4, n_z, depth)
        if staged:
            attn, ff = gather_first(jnp.concatenate([attn, vec], axis=1), ff)
        else:
            vec = lax.all_gather(vec, "dp", axis=0, tiled=True)
            attn = jnp.concatenate([gather_plain(attn, 4), jnp.concatenate([vec] * HALVES)], axis=1)
            attn = plain_pieces(attn)
            ff = plain_pieces(gather_plain(ff, 2))
        q, k, v, p, ho, hidden, vec, wa = attn_forward(place, frames, tokens, attn)
        if staged:
            ff = gather_last(ff, vec)
        mixed, gh, f_own, f_other, gv_two = feed_forward(
            place, live, hidden, cotangent, ho, vec, ff, out_dims
        )
        if staged:
            f_mine = scatter_core(f_own, f_other)
            gh = after(gh, f_mine)
            f_mine, f_got = scatter_plane(f_mine)
        grad_input, a_own, a_other = attn_backward(
            place, tokens, gh, q, k, v, p, wa, vec, gv_two, out_dims
        )
        if staged:
            a_mine = scatter_core(a_own, a_other)
            f_mine = after(scatter_add(f_mine, f_got), a_mine)
            f_mine, f_got = scatter_z(f_mine)
            a_mine, a_got = scatter_plane(a_mine)
            a_mine = after(scatter_add(a_mine, a_got), *f_got)
            gf = scatter_sum(f_mine, f_got)
            ga = scatter_sum(*scatter_z(a_mine))
        else:
            gf = scatter_plain(f_own, f_other, (FW, FW, HW))
            ga = scatter_plain(a_own, a_other, (HW,) * 3)
        wide = w_query.shape[1]
        tall = w_up.shape[1]
        gains = ga[:, 3 * wide :]
        return (
            mixed,
            grad_input,
            ga[:, :wide],
            ga[:, wide : 2 * wide],
            ga[:, 2 * wide : 3 * wide],
            gf[:, 2 * tall :].T,
            gf[:, :tall],
            gf[:, tall : 2 * tall].T,
            gains[:, 0],
            gains[:, 1],
            gains[:, 2],
            gains[:, 3],
        )

    return shards


def solution(mesh):
    rows = P(("dp", "mp"), None)
    wide, tall, dp = P("dp", "mp"), P("mp", "dp"), P("dp")
    return jax.shard_map(
        build(mesh),
        mesh=mesh,
        in_specs=(rows, rows, dp, dp, wide, wide, wide, tall, wide, tall, dp, dp, dp, dp),
        out_specs=(rows, rows, wide, wide, wide, tall, wide, tall, dp, dp, dp, dp),
        check_vma=False,
    )
```

```python
import jax
import jax.numpy as jnp
from jax import lax
from jax.experimental import pallas as pl
from jax.experimental.pallas import tpu as pltpu
from jax.sharding import PartitionSpec as P

D = 512
FF = 2048
HEAD = 64
FTOK = 8
SEQ = 48
HALVES = 2
HW = D // HALVES
FW = FF // HALVES
PAIR = 2 * HEAD
GC = 128
EPS = 1e-05
CHUNK = 256
BF = jnp.bfloat16
F32 = jnp.float32


def nn(a, b):
    return lax.dot_general(a, b, (((1,), (0,)), ((), ())), preferred_element_type=F32)


def nt(a, b):
    return lax.dot_general(a, b, (((1,), (1,)), ((), ())), preferred_element_type=F32)


def tn(a, b):
    return lax.dot_general(a, b, (((0,), (0,)), ((), ())), preferred_element_type=F32)


def norm_parts(rows):
    mean = jnp.mean(rows, axis=-1, keepdims=True)
    centered = rows - mean
    spread = jnp.mean(centered * centered, axis=-1, keepdims=True)
    rstd = lax.rsqrt(spread + EPS)
    return centered * rstd, rstd


def norm_back(n, rstd, gain, gy):
    gg = gy * gain
    first = jnp.mean(gg, axis=-1, keepdims=True)
    second = jnp.mean(gg * n, axis=-1, keepdims=True)
    return rstd * (gg - first - n * second)


def fold_rows(value):
    return jnp.sum(value.reshape(value.shape[0] // 8, 8, value.shape[1]), axis=0)


def per_head(rows):
    width = rows.shape[1]
    lane = lax.broadcasted_iota(jnp.int32, rows.shape, 1) // HEAD
    pad = jnp.zeros((HEAD - SEQ, width), rows.dtype)
    parts = []
    for h in range(width // HEAD):
        parts.append(jnp.where(lane == h, rows, jnp.zeros_like(rows)))
        parts.append(pad)
    return jnp.concatenate(parts, axis=0)


def pair_blocks(product):
    lane = lax.broadcasted_iota(jnp.int32, (SEQ, PAIR), 1)
    return jnp.where(lane < HEAD, product[:SEQ], product[HEAD : HEAD + SEQ])


def head_rows(rows):
    lane = lax.broadcasted_iota(jnp.int32, rows.shape, 1)
    zero = jnp.zeros_like(rows)
    return jnp.concatenate([jnp.where(lane < HEAD, rows, zero), jnp.where(lane < HEAD, zero, rows)], axis=0)


def pair_scores(left, right):
    right = jnp.concatenate([right, jnp.zeros((HEAD - SEQ, right.shape[1]), right.dtype)], axis=0)
    both = nt(head_rows(left), right)
    return jnp.concatenate([both[:SEQ], both[SEQ:]], axis=1)


def seq_slice(s, c, width):
    return (slice(s * SEQ, (s + 1) * SEQ), slice(c * width, (c + 1) * width))


def block_place(place, cr, xr, yr, zr):
    z, x, c, y = place[0], place[1], place[2], place[3]
    z = lax.rem(z - zr + place[4], place[4])
    return (y ^ yr, z * 4 + (x ^ xr) * 2 + (c ^ cr))


def load_pieces(place, pieces, metas, dst, sems):
    copies = []
    for piece, meta in zip(pieces, metas):
        depth = piece.shape[0] // len(meta)
        n_dp = D // depth
        for b, rel in enumerate(meta):
            m, dp = block_place(place, *rel)
            row = pl.multiple_of((m * n_dp + dp) * depth, depth)
            copy = pltpu.make_async_copy(
                piece.at[pl.ds(b * depth, depth), :], dst.at[pl.ds(row, depth), :], sems.at[len(copies)]
            )
            copy.start()
            copies.append(copy)
    return copies


def wait_all(copies):
    for copy in copies:
        copy.wait()


def store_blocks(place, acc, start, own_ref, other_ref):
    slots, n_z, depth, width = own_ref.shape
    n_dp = n_z * 4
    for core in range(2):

        @pl.when(place[2] == core)
        def _():
            for m in range(HALVES):
                for dp in range(n_dp):
                    z, x, c = dp // 4, (dp // 2) % 2, dp % 2
                    slot = (place[1] ^ x) + 2 * (place[3] ^ m)
                    back = lax.rem(z - place[0] + n_z, n_z)
                    rows = slice(dp * depth, (dp + 1) * depth)
                    ref = own_ref if c == core else other_ref
                    ref[slot, back, :, start : start + acc.shape[2]] = acc[m, rows, :].astype(BF)


def pack_kernel(q_ref, k_ref, v_ref, o_ref, u_ref, d_ref, vec_ref, attn_ref, ff_ref):
    at = 0
    for ref in (q_ref, k_ref, v_ref, o_ref):
        attn_ref[:, at : at + ref.shape[1]] = ref[...]
        at += ref.shape[1]
    vec = jnp.concatenate([vec_ref[...].astype(F32), jnp.zeros((GC - 4, vec_ref.shape[1]), F32)], axis=0)
    attn_ref[:, at:] = vec.T.astype(BF)
    ff_ref[:, : u_ref.shape[1]] = u_ref[...]
    ff_ref[:, u_ref.shape[1] :] = d_ref[...]


def attn_forward_kernel(place, frames, metas, x_ref, *refs):
    n = len(metas)
    pieces = refs[:n]
    qkvp_ref, ho_ref, hidden_ref, vec_ref, w_ref, s_ref, sems = refs[n:]
    q_ref, k_ref, v_ref, p_ref = (qkvp_ref.at[:, i * D : (i + 1) * D] for i in range(4))
    step = pl.program_id(0)
    seqs = x_ref.shape[0] // SEQ

    @pl.when(step == 0)
    def _():
        wait_all(load_pieces(place, pieces, metas, w_ref, sems))
        vec_ref[...] = w_ref[:D, 4 * HW :].astype(F32).T[:8]

    x = x_ref[...].astype(F32)
    n, _ = norm_parts(x)
    normed = (n * vec_ref[0:1] + vec_ref[1:2]).astype(BF)
    for m in range(HALVES):
        qkv = nn(normed, w_ref[m * D : (m + 1) * D, : 3 * HW]).astype(BF)
        cols = slice(m * HW, (m + 1) * HW)
        q_ref[:, cols] = qkv[:, :HW]
        k_ref[:, cols] = qkv[:, HW : 2 * HW]
        v_ref[:, cols] = qkv[:, 2 * HW :]
    for s in range(seqs):
        for m in range(HALVES):
            at = seq_slice(s, m, HW)
            s_ref[at] = nt(k_ref[at], per_head(q_ref[at]))
    key = lax.broadcasted_iota(jnp.int32, (SEQ, PAIR), 0)
    query = lax.broadcasted_iota(jnp.int32, (SEQ, PAIR), 1) % HEAD
    for s in range(seqs):
        allowed = (key <= query) & (key < frames[place[5] + step * seqs + s] * FTOK)
        for c in range(D // PAIR):
            at = seq_slice(s, c, PAIR)
            scores = jnp.where(allowed, s_ref[at] * HEAD**-0.5, -1000000000.0)
            expd = jnp.exp(scores - jnp.max(scores, axis=0, keepdims=True))
            p_ref[at] = (expd * (1.0 / jnp.sum(expd, axis=0, keepdims=True))).astype(BF)
    for s in range(seqs):
        for c in range(D // PAIR):
            at = seq_slice(s, c, PAIR)
            ho_ref[at] = pair_blocks(tn(p_ref[at], v_ref[at])).astype(BF)
    attended = nt(ho_ref[:, :HW], w_ref[:D, 3 * HW : 4 * HW]) + nt(ho_ref[:, HW:], w_ref[D:, 3 * HW : 4 * HW])
    hidden_ref[...] = x + attended


GELU_A = (2.0 / jnp.pi) ** 0.5
GELU_B = 0.044715


def feed_forward_kernel(place, live, metas, hidden_ref, cot_ref, ho_ref, vec_ref, *refs):
    n = len(metas)
    (
        mixed_ref, gh_ref, own_ref, other_ref, gv_ref,
        w_ref, accu_ref, accd_ref, acco_ref, gvacc_ref, act_ref, gup_ref, go_ref, sems,
    ) = refs[n:]
    step = pl.program_id(0)
    last = pl.num_programs(0) - 1
    rows = hidden_ref.shape[0]

    @pl.when(step == 0)
    def _():
        copies = load_pieces(place, refs[:n], metas, w_ref, sems)
        accu_ref[...] = jnp.zeros_like(accu_ref)
        accd_ref[...] = jnp.zeros_like(accd_ref)
        acco_ref[...] = jnp.zeros_like(acco_ref)
        gvacc_ref[...] = jnp.zeros_like(gvacc_ref)
        wait_all(copies)

    hidden = hidden_ref[...]
    n, rstd = norm_parts(hidden)
    normed = (n * vec_ref[2:3] + vec_ref[3:4]).astype(BF)
    row = lax.broadcasted_iota(jnp.int32, (rows, 1), 0) + step * rows
    go = jnp.where(row < (live[0] - place[5]) * SEQ, cot_ref[...].astype(F32), 0.0)
    go_ref[...] = go.astype(BF)
    for m in range(HALVES):
        for c in range(FW // CHUNK):
            depth = slice(m * D, (m + 1) * D)
            cols = slice(m * FW + c * CHUNK, m * FW + (c + 1) * CHUNK)
            up = nn(normed, w_ref[depth, c * CHUNK : (c + 1) * CHUNK])
            ga = nn(go_ref[...], w_ref[depth, FW + c * CHUNK : FW + (c + 1) * CHUNK])
            sq = up * up
            th = jnp.tanh(up * (GELU_A + (GELU_A * GELU_B) * sq))
            half = 0.5 + 0.5 * th
            act_ref[:, cols] = (up * half).astype(BF)
            slope = half + (0.5 * up) * (1.0 - th * th) * (GELU_A + (3.0 * GELU_A * GELU_B) * sq)
            gup_ref[:, cols] = (ga * slope).astype(BF)
    down = jnp.zeros((rows, D), F32)
    gy = jnp.zeros((rows, D), F32)
    for m in range(HALVES):
        cols = slice(m * FW, (m + 1) * FW)
        down += nt(act_ref[:, cols], w_ref[m * D : (m + 1) * D, FW:])
        gy += nt(gup_ref[:, cols], w_ref[m * D : (m + 1) * D, :FW])
        accu_ref[m] += tn(normed, gup_ref[:, cols])
        accd_ref[m] += tn(go_ref[...], act_ref[:, cols])
    mixed_ref[...] = (hidden + down).astype(BF)
    gh = go + norm_back(n, rstd, vec_ref[2:3], gy)
    gh_ref[...] = gh
    for m in range(HALVES):
        acco_ref[m] += tn(gh.astype(BF), ho_ref[:, m * HW : (m + 1) * HW])
    gvacc_ref[0] += fold_rows(gy * n)
    gvacc_ref[1] += fold_rows(gy)

    @pl.when(step == last)
    def _():
        store_blocks(place, accu_ref, 0, own_ref, other_ref)
        store_blocks(place, accd_ref, FW, own_ref, other_ref)
        store_blocks(place, acco_ref, 2 * FW, own_ref, other_ref)
        gv_ref[0:1] = jnp.sum(gvacc_ref[0], axis=0, keepdims=True)
        gv_ref[1:2] = jnp.sum(gvacc_ref[1], axis=0, keepdims=True)


def attn_backward_kernel(
    place, x_ref, gh_ref, qkvp_ref, w_ref, vec_ref, gvtwo_ref,
    gi_ref, own_ref, other_ref, acc_ref, gvacc_ref, gvec_ref, s_ref, ds_ref, dh_ref, dqkv_ref,
):
    step = pl.program_id(0)
    last = pl.num_programs(0) - 1
    seqs = x_ref.shape[0] // SEQ
    q_ref, k_ref, v_ref, p_ref = (qkvp_ref.at[:, i * D : (i + 1) * D] for i in range(4))

    @pl.when(step == 0)
    def _():
        acc_ref[...] = jnp.zeros_like(acc_ref)
        gvacc_ref[...] = jnp.zeros_like(gvacc_ref)

    gh = gh_ref[...]
    gat = gh.astype(BF)
    for m in range(HALVES):
        dh_ref[:, m * HW : (m + 1) * HW] = nn(gat, w_ref[m * D : (m + 1) * D, 3 * HW : 4 * HW]).astype(BF)
    for s in range(seqs):
        for c in range(D // PAIR):
            at = seq_slice(s, c, PAIR)
            base = 3 * HW * (c * PAIR // HW) + c * PAIR % HW
            s_ref[at] = pair_scores(v_ref[at], dh_ref[at])
            dqkv_ref[at[0], base + 2 * HW : base + 2 * HW + PAIR] = nn(p_ref[at], per_head(dh_ref[at])).astype(BF)
    for s in range(seqs):
        for c in range(D // PAIR):
            at = seq_slice(s, c, PAIR)
            probs = p_ref[at].astype(F32)
            gp = s_ref[at]
            delta = jnp.sum(probs * gp, axis=0, keepdims=True)
            ds_ref[at] = (probs * ((gp - delta) * HEAD**-0.5)).astype(BF)
    for s in range(seqs):
        for c in range(D // PAIR):
            at = seq_slice(s, c, PAIR)
            base = 3 * HW * (c * PAIR // HW) + c * PAIR % HW
            dqkv_ref[at[0], base + HW : base + HW + PAIR] = nn(ds_ref[at], per_head(q_ref[at])).astype(BF)
            dqkv_ref[at[0], base : base + PAIR] = pair_blocks(tn(ds_ref[at], k_ref[at])).astype(BF)
    n, rstd = norm_parts(x_ref[...].astype(F32))
    normed = (n * vec_ref[0:1] + vec_ref[1:2]).astype(BF)
    gy = jnp.zeros(x_ref.shape, F32)
    for m in range(HALVES):
        cols = slice(3 * HW * m, 3 * HW * (m + 1))
        gy += nt(dqkv_ref[:, cols], w_ref[m * D : (m + 1) * D, : 3 * HW])
        acc_ref[m] += tn(normed, dqkv_ref[:, cols])
    gi_ref[...] = gh + norm_back(n, rstd, vec_ref[0:1], gy)
    gvacc_ref[0] += fold_rows(gy * n)
    gvacc_ref[1] += fold_rows(gy)

    @pl.when(step == last)
    def _():
        store_blocks(place, acc_ref, 0, own_ref, other_ref)
        one = jnp.concatenate([jnp.sum(gvacc_ref[i], axis=0, keepdims=True) for i in range(2)], axis=0)
        rows = jnp.concatenate([one, gvtwo_ref[...], jnp.zeros((GC - 4, D), F32)], axis=0)
        for m in range(HALVES):
            gvec_ref[m] = rows.T
        store_blocks(place, gvec_ref, 3 * HW, own_ref, other_ref)


def step_rows(rows):
    return 16 * SEQ if rows % (16 * SEQ) == 0 else 8 * SEQ


def row_block(rows, width):
    return pl.BlockSpec((step_rows(rows), width), lambda i, *_: (i, 0))


def held(shape):
    return pl.BlockSpec(shape, lambda i, *_: (0,) * len(shape), pipeline_mode=pl.Buffered(1))


def shape(dims, dtype):
    return jax.ShapeDtypeStruct(dims, dtype)


def vmem(mib):
    return pltpu.CompilerParams(vmem_limit_bytes=mib * 1024 * 1024)


HBM = pl.BlockSpec(memory_space=pl.ANY)


def weight_dims(group):
    return (HALVES * D, group[0][0].shape[1])


def copy_sems(group):
    return pltpu.SemaphoreType.DMA((sum(len(meta) for meta in group[1]),))


def cost(flops, nbytes):
    return pl.CostEstimate(flops=flops, bytes_accessed=nbytes, transcendentals=0)


def pack(w_query, w_key, w_value, w_out, w_up, w_down, vec):
    depth = w_query.shape[0]
    return pl.pallas_call(
        pack_kernel,
        out_shape=[shape((depth, 4 * w_query.shape[1] + GC), BF), shape((depth, 2 * w_up.shape[1]), BF)],
        name="pack",
    )(w_query, w_key, w_value, w_out, w_up, w_down, vec)


def attn_forward(place, frames, tokens, group):
    rows = tokens.shape[0]
    dims = weight_dims(group)
    return pl.pallas_call(
        lambda place, frames, *refs: attn_forward_kernel(place, frames, group[1], *refs),
        grid_spec=pltpu.PrefetchScalarGridSpec(
            num_scalar_prefetch=2,
            grid=(rows // step_rows(rows),),
            in_specs=[row_block(rows, D)] + [HBM] * len(group[0]),
            out_specs=[row_block(rows, 4 * D), row_block(rows, D), row_block(rows, D), held((8, D)), held(dims)],
            scratch_shapes=[pltpu.VMEM((step_rows(rows), D), F32), copy_sems(group)],
        ),
        out_shape=[
            shape((rows, 4 * D), BF),
            shape((rows, D), BF),
            shape((rows, D), F32),
            shape((8, D), F32),
            shape(dims, BF),
        ],
        compiler_params=vmem(60),
        cost_estimate=cost(rows * D * D * 24, rows * D * 18),
        name="attn_forward",
    )(place, frames, tokens, *group[0])


def feed_forward(place, live, hidden, cotangent, ho, vec, group, out_dims):
    rows = hidden.shape[0]
    grads = out_dims + (2 * FW + HW,)
    dims = weight_dims(group)
    return pl.pallas_call(
        lambda place, live, *refs: feed_forward_kernel(place, live, group[1], *refs),
        grid_spec=pltpu.PrefetchScalarGridSpec(
            num_scalar_prefetch=2,
            grid=(rows // step_rows(rows),),
            in_specs=[row_block(rows, D)] * 3 + [held((8, D))] + [HBM] * len(group[0]),
            out_specs=[row_block(rows, D), row_block(rows, D), held(grads), held(grads), held((2, D))],
            scratch_shapes=[
                pltpu.VMEM(dims, BF),
                pltpu.VMEM((HALVES, D, FW), F32),
                pltpu.VMEM((HALVES, D, FW), F32),
                pltpu.VMEM((HALVES, D, HW), F32),
                pltpu.VMEM((2, 8, D), F32),
                pltpu.VMEM((step_rows(rows), FF), BF),
                pltpu.VMEM((step_rows(rows), FF), BF),
                pltpu.VMEM((step_rows(rows), D), BF),
                copy_sems(group),
            ],
        ),
        out_shape=[
            shape((rows, D), BF),
            shape((rows, D), F32),
            shape(grads, BF),
            shape(grads, BF),
            shape((2, D), F32),
        ],
        compiler_params=vmem(54),
        cost_estimate=cost(rows * D * FF * 12, rows * D * 12),
        name="feed_forward",
    )(place, live, hidden, cotangent, ho, vec, *group[0])


def attn_backward(place, tokens, gh, qkvp, w, vec, gv_two, out_dims):
    rows = tokens.shape[0]
    grads = out_dims + (3 * HW + GC,)
    return pl.pallas_call(
        attn_backward_kernel,
        grid_spec=pltpu.PrefetchScalarGridSpec(
            num_scalar_prefetch=1,
            grid=(rows // step_rows(rows),),
            in_specs=[row_block(rows, D)] * 2 + [row_block(rows, 4 * D), held(w.shape), held((8, D)), held((2, D))],
            out_specs=[row_block(rows, D), held(grads), held(grads)],
            scratch_shapes=[
                pltpu.VMEM((HALVES, D, 3 * HW), F32),
                pltpu.VMEM((2, 8, D), F32),
                pltpu.VMEM((HALVES, D, GC), F32),
                pltpu.VMEM((step_rows(rows), D), F32),
                pltpu.VMEM((step_rows(rows), D), BF),
                pltpu.VMEM((step_rows(rows), D), BF),
                pltpu.VMEM((step_rows(rows), 3 * D), BF),
            ],
        ),
        out_shape=[shape((rows, D), F32), shape(grads, BF), shape(grads, BF)],
        compiler_params=vmem(40),
        cost_estimate=cost(rows * D * D * 36, rows * D * 18),
        name="attn_backward",
    )(place, tokens, gh, qkvp, w, vec, gv_two)


def build(mesh):
    n_dp, n_mp = mesh.shape["dp"], mesh.shape["mp"]
    n_z = n_dp // 4
    depth = D // n_dp
    staged = n_mp == HALVES
    both = ("dp", "mp")
    PLANE = ((0, 0), (1, 0), (0, 1), (1, 1))

    def send(value, zr=0, xr=0, yr=0, cr=0):
        pairs = []
        for z in range(n_z):
            for x in range(2):
                for c in range(2):
                    for y in range(n_mp):
                        here = ((z * 2 + x) * 2 + c) * n_mp + y
                        there = ((((z + zr) % n_z) * 2 + (x ^ xr)) * 2 + (c ^ cr)) * n_mp + (y ^ yr)
                        pairs.append((here, there))
        return lax.ppermute(value, both, pairs)

    def along_z(value):
        return [value] + [send(value, zr=r) for r in range(1, n_z)]

    def across_plane(value):
        return [value] + [send(value, xr=x, yr=y) for x, y in PLANE[1:]]

    def both_cores(pieces):
        return pieces + [send(piece, cr=1) for piece in pieces]

    def stack(blocks):
        return jnp.concatenate(blocks, axis=0)

    Z_FIRST = tuple(tuple((c, x, y, z) for z in range(n_z)) for c in range(2) for x, y in PLANE)
    PLANE_FIRST = tuple(tuple((c, x, y, z) for x, y in PLANE) for c in range(2) for z in range(n_z))

    def after(value, *others):
        return lax.optimization_barrier((value,) + others)[0]

    def gather_first(attn, ff, place):
        attn_z = along_z(attn)
        attn_plane = across_plane(after(stack(attn_z), place))
        ff_z = along_z(after(ff, attn_z[-1]))
        ff_plane = across_plane(after(stack(ff_z), attn_plane[-1]))
        return (both_cores(attn_plane), Z_FIRST), ff_plane

    def gather_last(ff_plane, done):
        ff_plane = ff_plane[:1] + [after(piece, done) for piece in ff_plane[1:]]
        return both_cores(ff_plane), Z_FIRST

    def gather_plain(block, parts):
        out = lax.all_gather(block, ("mp", "dp"), axis=0, tiled=True)
        out = out.reshape(HALVES, n_mp // HALVES, D, parts, -1)
        return out.transpose(0, 2, 3, 1, 4).reshape(HALVES * D, -1)

    def plain_pieces(whole):
        z, x, c = lax.axis_index("dp") // 4, (lax.axis_index("dp") // 2) % 2, lax.axis_index("dp") % 2
        y = lax.axis_index("mp") % HALVES
        blocks = whole.reshape(HALVES, n_z, 2, 2, depth, -1)
        index = lambda n, at: (at - jnp.arange(n)) % n
        blocks = blocks[:, index(n_z, z)]
        blocks = blocks[y ^ jnp.arange(2)][:, :, x ^ jnp.arange(2)][:, :, :, c ^ jnp.arange(2)]
        blocks = blocks.transpose(3, 0, 2, 1, 4, 5).reshape(8, n_z * depth, -1)
        return [blocks[i] for i in range(8)], Z_FIRST

    def scatter_core(own, other):
        got = send(other, cr=1)
        return [(own[slot].astype(F32) + got[slot].astype(F32)).astype(BF) for slot in range(4)]

    def scatter_plane(mine):
        return mine[0], [send(mine[x + 2 * y], xr=x, yr=y) for x, y in PLANE[1:]]

    def scatter_add(mine, got):
        got = [part.astype(F32) for part in got]
        return ((mine.astype(F32) + got[0]) + (got[1] + got[2])).astype(BF)

    def scatter_z(mine):
        return mine[0], [send(mine[r], zr=r) for r in range(1, n_z)]

    def scatter_sum(mine, got):
        total = mine.astype(F32)
        for part in got:
            total += part.astype(F32)
        return total

    def scatter_plain(own, other, parts):
        z, x, c = lax.axis_index("dp") // 4, (lax.axis_index("dp") // 2) % 2, lax.axis_index("dp") % 2
        y = lax.axis_index("mp") % HALVES
        blocks = jnp.stack([own, other]).reshape(2, 2, 2, n_z, depth, -1)
        blocks = blocks[c ^ jnp.arange(2)][:, y ^ jnp.arange(2)][:, :, x ^ jnp.arange(2)]
        blocks = blocks[:, :, :, (jnp.arange(n_z) - z) % n_z]
        blocks = blocks.transpose(1, 3, 2, 0, 4, 5).reshape(HALVES, D, -1)
        main, start = [], 0
        for part in parts:
            cut = blocks[:, :, start : start + part].reshape(HALVES, D, n_mp // HALVES, -1)
            main.append(cut.transpose(0, 2, 1, 3).reshape(n_mp, D, -1))
            start += part
        main = jnp.concatenate(main, axis=2)
        tail = jnp.broadcast_to(blocks[:1, :, start:], (n_mp, D, blocks.shape[2] - start))
        flat = jnp.concatenate([main, tail], axis=2).reshape(n_mp * D, -1)
        return lax.psum_scatter(flat, ("mp", "dp"), scatter_dimension=0, tiled=True).astype(F32)

    def shards(
        tokens, cotangent, frame_count, live_count, w_query, w_key, w_value, w_out, w_up, w_down,
        gain_one, shift_one, gain_two, shift_two,
    ):
        dp, mp = lax.axis_index("dp"), lax.axis_index("mp")
        seqs = tokens.shape[0] // SEQ
        place = jnp.stack([dp // 4, (dp // 2) % 2, dp % 2, mp % HALVES, jnp.int32(n_z), mp * seqs])
        place = place.astype(jnp.int32)
        vec = jnp.stack([gain_one, shift_one, gain_two, shift_two])
        out_dims = (4, n_z, depth)
        if staged:
            attn, ff = gather_first(*pack(w_query, w_key, w_value, w_out.T, w_up, w_down.T, vec), place)
        else:
            vec = lax.all_gather(jnp.pad(vec.T, ((0, 0), (0, GC - 4))), "dp", axis=0, tiled=True)
            attn = gather_plain(jnp.concatenate([w_query, w_key, w_value, w_out.T], axis=1), 4)
            attn = plain_pieces(jnp.concatenate([attn, jnp.concatenate([vec] * HALVES)], axis=1))
            ff = plain_pieces(gather_plain(jnp.concatenate([w_up, w_down.T], axis=1), 2))
        qkvp, ho, hidden, vec, wa = attn_forward(place, frame_count, tokens, attn)
        if staged:
            ff = gather_last(ff, vec)
        mixed, gh, f_own, f_other, gv_two = feed_forward(
            place, live_count, hidden, cotangent, ho, vec, ff, out_dims
        )
        if staged:
            f_mine = scatter_core(f_own, f_other)
            gh = after(gh, *f_mine[1:])
            f_mine, f_got = scatter_plane(f_mine)
        grad_input, a_own, a_other = attn_backward(
            place, tokens, gh, qkvp, wa, vec, gv_two, out_dims
        )
        if staged:
            a_mine = scatter_core(a_own, a_other)
            f_mine = after(scatter_add(f_mine, f_got), *a_mine[1:])
            f_mine, f_got = scatter_z(f_mine)
            a_mine, a_got = scatter_plane(a_mine)
            a_mine = after(scatter_add(a_mine, a_got), *f_got)
            gf = scatter_sum(f_mine, f_got)
            ga = scatter_sum(*scatter_z(a_mine))
        else:
            gf = scatter_plain(f_own, f_other, (FW, FW, HW))
            ga = scatter_plain(a_own, a_other, (HW,) * 3)
        wide = w_query.shape[1]
        tall = w_up.shape[1]
        gains = ga[:, 3 * wide :]
        return (
            mixed,
            grad_input,
            ga[:, :wide],
            ga[:, wide : 2 * wide],
            ga[:, 2 * wide : 3 * wide],
            gf[:, 2 * tall :].T,
            gf[:, :tall],
            gf[:, tall : 2 * tall].T,
            gains[:, 0],
            gains[:, 1],
            gains[:, 2],
            gains[:, 3],
        )

    return shards


def solution(mesh):
    rows = P(("dp", "mp"), None)
    wide, tall, dp = P("dp", "mp"), P("mp", "dp"), P("dp")
    return jax.shard_map(
        build(mesh),
        mesh=mesh,
        in_specs=(rows, rows, dp, dp, wide, wide, wide, tall, wide, tall, dp, dp, dp, dp),
        out_specs=(rows, rows, wide, wide, wide, tall, wide, tall, dp, dp, dp, dp),
        check_vma=False,
    )
```

```python
import jax
import jax.numpy as jnp
from jax import lax
from jax.experimental import pallas as pl
from jax.experimental.pallas import tpu as pltpu
from jax.sharding import PartitionSpec as P

D = 512
FF = 2048
HEAD = 64
FTOK = 8
SEQ = 48
HALVES = 2
HW = D // HALVES
FW = FF // HALVES
PAIR = 2 * HEAD
GC = 128
EPS = 1e-05
CHUNK = 256
BF = jnp.bfloat16
F32 = jnp.float32


def nn(a, b):
    return lax.dot_general(a, b, (((1,), (0,)), ((), ())), preferred_element_type=F32)


def nt(a, b):
    return lax.dot_general(a, b, (((1,), (1,)), ((), ())), preferred_element_type=F32)


def tn(a, b):
    return lax.dot_general(a, b, (((0,), (0,)), ((), ())), preferred_element_type=F32)


def norm_parts(rows):
    mean = jnp.mean(rows, axis=-1, keepdims=True)
    centered = rows - mean
    spread = jnp.mean(centered * centered, axis=-1, keepdims=True)
    rstd = lax.rsqrt(spread + EPS)
    return centered * rstd, rstd


def norm_back(n, rstd, gain, gy):
    gg = gy * gain
    first = jnp.mean(gg, axis=-1, keepdims=True)
    second = jnp.mean(gg * n, axis=-1, keepdims=True)
    return rstd * (gg - first - n * second)


def fold_rows(value):
    return jnp.sum(value.reshape(value.shape[0] // 8, 8, value.shape[1]), axis=0)


def per_head(rows):
    width = rows.shape[1]
    lane = lax.broadcasted_iota(jnp.int32, rows.shape, 1) // HEAD
    pad = jnp.zeros((HEAD - SEQ, width), rows.dtype)
    parts = []
    for h in range(width // HEAD):
        parts.append(jnp.where(lane == h, rows, jnp.zeros_like(rows)))
        parts.append(pad)
    return jnp.concatenate(parts, axis=0)


def pair_blocks(product):
    lane = lax.broadcasted_iota(jnp.int32, (SEQ, PAIR), 1)
    return jnp.where(lane < HEAD, product[:SEQ], product[HEAD : HEAD + SEQ])


def head_rows(rows):
    lane = lax.broadcasted_iota(jnp.int32, rows.shape, 1)
    zero = jnp.zeros_like(rows)
    return jnp.concatenate([jnp.where(lane < HEAD, rows, zero), jnp.where(lane < HEAD, zero, rows)], axis=0)


def pair_scores(left, right):
    right = jnp.concatenate([right, jnp.zeros((HEAD - SEQ, right.shape[1]), right.dtype)], axis=0)
    both = nt(head_rows(left), right)
    return jnp.concatenate([both[:SEQ], both[SEQ:]], axis=1)


def seq_slice(s, c, width):
    return (slice(s * SEQ, (s + 1) * SEQ), slice(c * width, (c + 1) * width))


def block_place(place, cr, xr, yr, zr):
    z, x, c, y = place[0], place[1], place[2], place[3]
    z = lax.rem(z - zr + place[4], place[4])
    return (y ^ yr, z * 4 + (x ^ xr) * 2 + (c ^ cr))


def load_pieces(place, pieces, metas, dst, sems):
    copies = []
    for piece, meta in zip(pieces, metas):
        depth = piece.shape[0] // len(meta)
        n_dp = D // depth
        for b, rel in enumerate(meta):
            m, dp = block_place(place, *rel)
            row = pl.multiple_of((m * n_dp + dp) * depth, depth)
            copy = pltpu.make_async_copy(
                piece.at[pl.ds(b * depth, depth), :], dst.at[pl.ds(row, depth), :], sems.at[len(copies)]
            )
            copy.start()
            copies.append(copy)
    return copies


def wait_all(copies):
    for copy in copies:
        copy.wait()


def store_blocks(place, acc, start, own_ref, other_ref):
    slots, n_z, depth, width = own_ref.shape
    n_dp = n_z * 4
    for core in range(2):

        @pl.when(place[2] == core)
        def _():
            for m in range(HALVES):
                for dp in range(n_dp):
                    z, x, c = dp // 4, (dp // 2) % 2, dp % 2
                    slot = (place[1] ^ x) + 2 * (place[3] ^ m)
                    back = lax.rem(z - place[0] + n_z, n_z)
                    rows = slice(dp * depth, (dp + 1) * depth)
                    ref = own_ref if c == core else other_ref
                    ref[slot, back, :, start : start + acc.shape[2]] = acc[m, rows, :].astype(BF)


def pack_kernel(q_ref, k_ref, v_ref, o_ref, u_ref, d_ref, vec_ref, attn_ref, ff_ref):
    at = 0
    for ref in (q_ref, k_ref, v_ref, o_ref):
        attn_ref[:, at : at + ref.shape[1]] = ref[...]
        at += ref.shape[1]
    vec = jnp.concatenate([vec_ref[...].astype(F32), jnp.zeros((GC - 4, vec_ref.shape[1]), F32)], axis=0)
    attn_ref[:, at:] = vec.T.astype(BF)
    ff_ref[:, : u_ref.shape[1]] = u_ref[...]
    ff_ref[:, u_ref.shape[1] :] = d_ref[...]


def attn_forward_kernel(place, frames, metas, x_ref, *refs):
    n = len(metas)
    pieces = refs[:n]
    qkvp_ref, ho_ref, hidden_ref, vec_ref, w_ref, s_ref, sems = refs[n:]
    q_ref, k_ref, v_ref, p_ref = (qkvp_ref.at[:, i * D : (i + 1) * D] for i in range(4))
    step = pl.program_id(0)
    seqs = x_ref.shape[0] // SEQ

    @pl.when(step == 0)
    def _():
        wait_all(load_pieces(place, pieces, metas, w_ref, sems))
        vec_ref[...] = w_ref[:D, 4 * HW :].astype(F32).T[:8]

    x = x_ref[...].astype(F32)
    n, _ = norm_parts(x)
    normed = (n * vec_ref[0:1] + vec_ref[1:2]).astype(BF)
    for m in range(HALVES):
        cols = slice(m * HW, (m + 1) * HW)
        for i, ref in enumerate((q_ref, k_ref)):
            ref[:, cols] = nn(normed, w_ref[m * D : (m + 1) * D, i * HW : (i + 1) * HW]).astype(BF)
    for s in range(seqs):
        for c in range(D // PAIR):
            at = seq_slice(s, c, PAIR)
            s_ref[at] = pair_scores(k_ref[at], q_ref[at])
    for m in range(HALVES):
        v_ref[:, m * HW : (m + 1) * HW] = nn(normed, w_ref[m * D : (m + 1) * D, 2 * HW : 3 * HW]).astype(BF)
    key = lax.broadcasted_iota(jnp.int32, (SEQ, PAIR), 0)
    query = lax.broadcasted_iota(jnp.int32, (SEQ, PAIR), 1) % HEAD
    for s in range(seqs):
        allowed = (key <= query) & (key < frames[place[5] + step * seqs + s] * FTOK)
        for c in range(D // PAIR):
            at = seq_slice(s, c, PAIR)
            scores = jnp.where(allowed, s_ref[at] * HEAD**-0.5, -1000000000.0)
            expd = jnp.exp(scores - jnp.max(scores, axis=0, keepdims=True))
            p_ref[at] = (expd * (1.0 / jnp.sum(expd, axis=0, keepdims=True))).astype(BF)
    for s in range(seqs):
        for c in range(D // PAIR):
            at = seq_slice(s, c, PAIR)
            ho_ref[at] = pair_blocks(tn(p_ref[at], v_ref[at])).astype(BF)
    attended = nt(ho_ref[:, :HW], w_ref[:D, 3 * HW : 4 * HW]) + nt(ho_ref[:, HW:], w_ref[D:, 3 * HW : 4 * HW])
    hidden_ref[...] = x + attended


GELU_A = (2.0 / jnp.pi) ** 0.5
GELU_B = 0.044715


def feed_forward_kernel(place, live, metas, hidden_ref, cot_ref, ho_ref, vec_ref, *refs):
    n = len(metas)
    (
        mixed_ref, gh_ref, own_ref, other_ref, gv_ref,
        w_ref, accu_ref, accd_ref, acco_ref, gvacc_ref, act_ref, gup_ref, go_ref, sems,
    ) = refs[n:]
    step = pl.program_id(0)
    last = pl.num_programs(0) - 1
    rows = hidden_ref.shape[0]

    @pl.when(step == 0)
    def _():
        copies = load_pieces(place, refs[:n], metas, w_ref, sems)
        accu_ref[...] = jnp.zeros_like(accu_ref)
        accd_ref[...] = jnp.zeros_like(accd_ref)
        acco_ref[...] = jnp.zeros_like(acco_ref)
        gvacc_ref[...] = jnp.zeros_like(gvacc_ref)
        wait_all(copies)

    hidden = hidden_ref[...]
    n, rstd = norm_parts(hidden)
    normed = (n * vec_ref[2:3] + vec_ref[3:4]).astype(BF)
    row = lax.broadcasted_iota(jnp.int32, (rows, 1), 0) + step * rows
    go = jnp.where(row < (live[0] - place[5]) * SEQ, cot_ref[...].astype(F32), 0.0)
    go_ref[...] = go.astype(BF)
    for m in range(HALVES):
        for c in range(FW // CHUNK):
            depth = slice(m * D, (m + 1) * D)
            cols = slice(m * FW + c * CHUNK, m * FW + (c + 1) * CHUNK)
            up = nn(normed, w_ref[depth, c * CHUNK : (c + 1) * CHUNK])
            ga = nn(go_ref[...], w_ref[depth, FW + c * CHUNK : FW + (c + 1) * CHUNK])
            sq = up * up
            th = jnp.tanh(up * (GELU_A + (GELU_A * GELU_B) * sq))
            half = 0.5 + 0.5 * th
            act_ref[:, cols] = (up * half).astype(BF)
            slope = half + (0.5 * up) * (1.0 - th * th) * (GELU_A + (3.0 * GELU_A * GELU_B) * sq)
            gup_ref[:, cols] = (ga * slope).astype(BF)
    down = jnp.zeros((rows, D), F32)
    gy = jnp.zeros((rows, D), F32)
    for m in range(HALVES):
        cols = slice(m * FW, (m + 1) * FW)
        down += nt(act_ref[:, cols], w_ref[m * D : (m + 1) * D, FW:])
        gy += nt(gup_ref[:, cols], w_ref[m * D : (m + 1) * D, :FW])
        accu_ref[m] += tn(normed, gup_ref[:, cols])
        accd_ref[m] += tn(go_ref[...], act_ref[:, cols])
    mixed_ref[...] = (hidden + down).astype(BF)
    gh = go + norm_back(n, rstd, vec_ref[2:3], gy)
    gh_ref[...] = gh
    for m in range(HALVES):
        acco_ref[m] += tn(gh_ref[...].astype(BF), ho_ref[:, m * HW : (m + 1) * HW])
    gvacc_ref[0] += fold_rows(gy * n)
    gvacc_ref[1] += fold_rows(gy)

    @pl.when(step == last)
    def _():
        store_blocks(place, accu_ref, 0, own_ref, other_ref)
        store_blocks(place, accd_ref, FW, own_ref, other_ref)
        store_blocks(place, acco_ref, 2 * FW, own_ref, other_ref)
        gv_ref[0:1] = jnp.sum(gvacc_ref[0], axis=0, keepdims=True)
        gv_ref[1:2] = jnp.sum(gvacc_ref[1], axis=0, keepdims=True)


def attn_backward_kernel(
    place, x_ref, gh_ref, qkvp_ref, w_ref, vec_ref, gvtwo_ref,
    gi_ref, own_ref, other_ref, acc_ref, gvacc_ref, gvec_ref, s_ref, ds_ref, dh_ref, dqkv_ref,
):
    step = pl.program_id(0)
    last = pl.num_programs(0) - 1
    seqs = x_ref.shape[0] // SEQ
    q_ref, k_ref, v_ref, p_ref = (qkvp_ref.at[:, i * D : (i + 1) * D] for i in range(4))

    @pl.when(step == 0)
    def _():
        acc_ref[...] = jnp.zeros_like(acc_ref)
        gvacc_ref[...] = jnp.zeros_like(gvacc_ref)

    gh = gh_ref[...]
    gat = gh.astype(BF)
    for m in range(HALVES):
        dh_ref[:, m * HW : (m + 1) * HW] = nn(gat, w_ref[m * D : (m + 1) * D, 3 * HW : 4 * HW]).astype(BF)
    for s in range(seqs):
        for c in range(D // PAIR):
            at = seq_slice(s, c, PAIR)
            base = 3 * HW * (c * PAIR // HW) + c * PAIR % HW
            s_ref[at] = pair_scores(v_ref[at], dh_ref[at])
            dqkv_ref[at[0], base + 2 * HW : base + 2 * HW + PAIR] = nn(p_ref[at], per_head(dh_ref[at])).astype(BF)
    for s in range(seqs):
        for c in range(D // PAIR):
            at = seq_slice(s, c, PAIR)
            probs = p_ref[at].astype(F32)
            gp = s_ref[at]
            delta = jnp.sum(probs * gp, axis=0, keepdims=True)
            ds_ref[at] = (probs * ((gp - delta) * HEAD**-0.5)).astype(BF)
    for s in range(seqs):
        for c in range(D // PAIR):
            at = seq_slice(s, c, PAIR)
            base = 3 * HW * (c * PAIR // HW) + c * PAIR % HW
            dqkv_ref[at[0], base + HW : base + HW + PAIR] = nn(ds_ref[at], per_head(q_ref[at])).astype(BF)
            dqkv_ref[at[0], base : base + PAIR] = pair_blocks(tn(ds_ref[at], k_ref[at])).astype(BF)
    n, rstd = norm_parts(x_ref[...].astype(F32))
    normed = (n * vec_ref[0:1] + vec_ref[1:2]).astype(BF)
    gy = jnp.zeros(x_ref.shape, F32)
    for m in range(HALVES):
        cols = slice(3 * HW * m, 3 * HW * (m + 1))
        gy += nt(dqkv_ref[:, cols], w_ref[m * D : (m + 1) * D, : 3 * HW])
        acc_ref[m] += tn(normed, dqkv_ref[:, cols])
    gi_ref[...] = gh + norm_back(n, rstd, vec_ref[0:1], gy)
    gvacc_ref[0] += fold_rows(gy * n)
    gvacc_ref[1] += fold_rows(gy)

    @pl.when(step == last)
    def _():
        store_blocks(place, acc_ref, 0, own_ref, other_ref)
        one = jnp.concatenate([jnp.sum(gvacc_ref[i], axis=0, keepdims=True) for i in range(2)], axis=0)
        rows = jnp.concatenate([one, gvtwo_ref[...], jnp.zeros((GC - 4, D), F32)], axis=0)
        for m in range(HALVES):
            gvec_ref[m] = rows.T
        store_blocks(place, gvec_ref, 3 * HW, own_ref, other_ref)


def step_rows(rows):
    return 16 * SEQ if rows % (16 * SEQ) == 0 else 8 * SEQ


def row_block(rows, width):
    return pl.BlockSpec((step_rows(rows), width), lambda i, *_: (i, 0))


def held(shape):
    return pl.BlockSpec(shape, lambda i, *_: (0,) * len(shape), pipeline_mode=pl.Buffered(1))


def shape(dims, dtype):
    return jax.ShapeDtypeStruct(dims, dtype)


def vmem(mib):
    return pltpu.CompilerParams(vmem_limit_bytes=mib * 1024 * 1024)


HBM = pl.BlockSpec(memory_space=pl.ANY)


def weight_dims(group):
    return (HALVES * D, group[0][0].shape[1])


def copy_sems(group):
    return pltpu.SemaphoreType.DMA((sum(len(meta) for meta in group[1]),))


def cost(flops, nbytes):
    return pl.CostEstimate(flops=flops, bytes_accessed=nbytes, transcendentals=0)


def pack(w_query, w_key, w_value, w_out, w_up, w_down, vec):
    depth = w_query.shape[0]
    return pl.pallas_call(
        pack_kernel,
        out_shape=[shape((depth, 4 * w_query.shape[1] + GC), BF), shape((depth, 2 * w_up.shape[1]), BF)],
        name="pack",
    )(w_query, w_key, w_value, w_out, w_up, w_down, vec)


def attn_forward(place, frames, tokens, group):
    rows = tokens.shape[0]
    dims = weight_dims(group)
    return pl.pallas_call(
        lambda place, frames, *refs: attn_forward_kernel(place, frames, group[1], *refs),
        grid_spec=pltpu.PrefetchScalarGridSpec(
            num_scalar_prefetch=2,
            grid=(rows // step_rows(rows),),
            in_specs=[row_block(rows, D)] + [HBM] * len(group[0]),
            out_specs=[row_block(rows, 4 * D), row_block(rows, D), row_block(rows, D), held((8, D)), held(dims)],
            scratch_shapes=[pltpu.VMEM((step_rows(rows), D), F32), copy_sems(group)],
        ),
        out_shape=[
            shape((rows, 4 * D), BF),
            shape((rows, D), BF),
            shape((rows, D), F32),
            shape((8, D), F32),
            shape(dims, BF),
        ],
        compiler_params=vmem(60),
        cost_estimate=cost(rows * D * D * 24, rows * D * 18),
        name="attn_forward",
    )(place, frames, tokens, *group[0])


def feed_forward(place, live, hidden, cotangent, ho, vec, group, out_dims):
    rows = hidden.shape[0]
    grads = out_dims + (2 * FW + HW,)
    dims = weight_dims(group)
    return pl.pallas_call(
        lambda place, live, *refs: feed_forward_kernel(place, live, group[1], *refs),
        grid_spec=pltpu.PrefetchScalarGridSpec(
            num_scalar_prefetch=2,
            grid=(rows // step_rows(rows),),
            in_specs=[row_block(rows, D)] * 3 + [held((8, D))] + [HBM] * len(group[0]),
            out_specs=[row_block(rows, D), row_block(rows, D), held(grads), held(grads), held((2, D))],
            scratch_shapes=[
                pltpu.VMEM(dims, BF),
                pltpu.VMEM((HALVES, D, FW), F32),
                pltpu.VMEM((HALVES, D, FW), F32),
                pltpu.VMEM((HALVES, D, HW), F32),
                pltpu.VMEM((2, 8, D), F32),
                pltpu.VMEM((step_rows(rows), FF), BF),
                pltpu.VMEM((step_rows(rows), FF), BF),
                pltpu.VMEM((step_rows(rows), D), BF),
                copy_sems(group),
            ],
        ),
        out_shape=[
            shape((rows, D), BF),
            shape((rows, D), F32),
            shape(grads, BF),
            shape(grads, BF),
            shape((2, D), F32),
        ],
        compiler_params=vmem(54),
        cost_estimate=cost(rows * D * FF * 12, rows * D * 12),
        name="feed_forward",
    )(place, live, hidden, cotangent, ho, vec, *group[0])


def attn_backward(place, tokens, gh, qkvp, w, vec, gv_two, out_dims):
    rows = tokens.shape[0]
    grads = out_dims + (3 * HW + GC,)
    return pl.pallas_call(
        attn_backward_kernel,
        grid_spec=pltpu.PrefetchScalarGridSpec(
            num_scalar_prefetch=1,
            grid=(rows // step_rows(rows),),
            in_specs=[row_block(rows, D)] * 2 + [row_block(rows, 4 * D), held(w.shape), held((8, D)), held((2, D))],
            out_specs=[row_block(rows, D), held(grads), held(grads)],
            scratch_shapes=[
                pltpu.VMEM((HALVES, D, 3 * HW), F32),
                pltpu.VMEM((2, 8, D), F32),
                pltpu.VMEM((HALVES, D, GC), F32),
                pltpu.VMEM((step_rows(rows), D), F32),
                pltpu.VMEM((step_rows(rows), D), BF),
                pltpu.VMEM((step_rows(rows), D), BF),
                pltpu.VMEM((step_rows(rows), 3 * D), BF),
            ],
        ),
        out_shape=[shape((rows, D), F32), shape(grads, BF), shape(grads, BF)],
        compiler_params=vmem(40),
        cost_estimate=cost(rows * D * D * 36, rows * D * 18),
        name="attn_backward",
    )(place, tokens, gh, qkvp, w, vec, gv_two)


def build(mesh):
    n_dp, n_mp = mesh.shape["dp"], mesh.shape["mp"]
    n_z = n_dp // 4
    depth = D // n_dp
    staged = n_mp == HALVES
    both = ("dp", "mp")
    PLANE = ((0, 0), (1, 0), (0, 1), (1, 1))

    def send(value, zr=0, xr=0, yr=0, cr=0):
        pairs = []
        for z in range(n_z):
            for x in range(2):
                for c in range(2):
                    for y in range(n_mp):
                        here = ((z * 2 + x) * 2 + c) * n_mp + y
                        there = ((((z + zr) % n_z) * 2 + (x ^ xr)) * 2 + (c ^ cr)) * n_mp + (y ^ yr)
                        pairs.append((here, there))
        return lax.ppermute(value, both, pairs)

    def along_z(value):
        return [value] + [send(value, zr=r) for r in range(1, n_z)]

    def across_plane(value):
        return [value] + [send(value, xr=x, yr=y) for x, y in PLANE[1:]]

    def both_cores(pieces):
        return pieces + [send(piece, cr=1) for piece in pieces]

    def stack(blocks):
        return jnp.concatenate(blocks, axis=0)

    Z_FIRST = tuple(tuple((c, x, y, z) for z in range(n_z)) for c in range(2) for x, y in PLANE)
    PLANE_FIRST = tuple(tuple((c, x, y, z) for x, y in PLANE) for c in range(2) for z in range(n_z))

    def after(value, *others):
        return lax.optimization_barrier((value,) + others)[0]

    def gather_first(attn, ff, place):
        attn_z = along_z(attn)
        attn_plane = across_plane(after(stack(attn_z), place))
        ff_z = along_z(after(ff, attn_z[-1]))
        ff_plane = across_plane(after(stack(ff_z), attn_plane[-1]))
        return (both_cores(attn_plane), Z_FIRST), ff_plane

    def gather_last(ff_plane, done):
        ff_plane = ff_plane[:1] + [after(piece, done) for piece in ff_plane[1:]]
        return both_cores(ff_plane), Z_FIRST

    def gather_plain(block, parts):
        out = lax.all_gather(block, ("mp", "dp"), axis=0, tiled=True)
        out = out.reshape(HALVES, n_mp // HALVES, D, parts, -1)
        return out.transpose(0, 2, 3, 1, 4).reshape(HALVES * D, -1)

    def plain_pieces(whole):
        z, x, c = lax.axis_index("dp") // 4, (lax.axis_index("dp") // 2) % 2, lax.axis_index("dp") % 2
        y = lax.axis_index("mp") % HALVES
        blocks = whole.reshape(HALVES, n_z, 2, 2, depth, -1)
        index = lambda n, at: (at - jnp.arange(n)) % n
        blocks = blocks[:, index(n_z, z)]
        blocks = blocks[y ^ jnp.arange(2)][:, :, x ^ jnp.arange(2)][:, :, :, c ^ jnp.arange(2)]
        blocks = blocks.transpose(3, 0, 2, 1, 4, 5).reshape(8, n_z * depth, -1)
        return [blocks[i] for i in range(8)], Z_FIRST

    def scatter_core(own, other):
        got = send(other, cr=1)
        return [(own[slot].astype(F32) + got[slot].astype(F32)).astype(BF) for slot in range(4)]

    def scatter_plane(mine):
        return mine[0], [send(mine[x + 2 * y], xr=x, yr=y) for x, y in PLANE[1:]]

    def scatter_add(mine, got):
        got = [part.astype(F32) for part in got]
        return ((mine.astype(F32) + got[0]) + (got[1] + got[2])).astype(BF)

    def scatter_z(mine):
        return mine[0], [send(mine[r], zr=r) for r in range(1, n_z)]

    def scatter_sum(mine, got):
        total = mine.astype(F32)
        for part in got:
            total += part.astype(F32)
        return total

    def scatter_plain(own, other, parts):
        z, x, c = lax.axis_index("dp") // 4, (lax.axis_index("dp") // 2) % 2, lax.axis_index("dp") % 2
        y = lax.axis_index("mp") % HALVES
        blocks = jnp.stack([own, other]).reshape(2, 2, 2, n_z, depth, -1)
        blocks = blocks[c ^ jnp.arange(2)][:, y ^ jnp.arange(2)][:, :, x ^ jnp.arange(2)]
        blocks = blocks[:, :, :, (jnp.arange(n_z) - z) % n_z]
        blocks = blocks.transpose(1, 3, 2, 0, 4, 5).reshape(HALVES, D, -1)
        main, start = [], 0
        for part in parts:
            cut = blocks[:, :, start : start + part].reshape(HALVES, D, n_mp // HALVES, -1)
            main.append(cut.transpose(0, 2, 1, 3).reshape(n_mp, D, -1))
            start += part
        main = jnp.concatenate(main, axis=2)
        tail = jnp.broadcast_to(blocks[:1, :, start:], (n_mp, D, blocks.shape[2] - start))
        flat = jnp.concatenate([main, tail], axis=2).reshape(n_mp * D, -1)
        return lax.psum_scatter(flat, ("mp", "dp"), scatter_dimension=0, tiled=True).astype(F32)

    def shards(
        tokens, cotangent, frame_count, live_count, w_query, w_key, w_value, w_out, w_up, w_down,
        gain_one, shift_one, gain_two, shift_two,
    ):
        dp, mp = lax.axis_index("dp"), lax.axis_index("mp")
        seqs = tokens.shape[0] // SEQ
        place = jnp.stack([dp // 4, (dp // 2) % 2, dp % 2, mp % HALVES, jnp.int32(n_z), mp * seqs])
        place = place.astype(jnp.int32)
        vec = jnp.stack([gain_one, shift_one, gain_two, shift_two])
        out_dims = (4, n_z, depth)
        if staged:
            attn, ff = gather_first(*pack(w_query, w_key, w_value, w_out.T, w_up, w_down.T, vec), place)
        else:
            vec = lax.all_gather(jnp.pad(vec.T, ((0, 0), (0, GC - 4))), "dp", axis=0, tiled=True)
            attn = gather_plain(jnp.concatenate([w_query, w_key, w_value, w_out.T], axis=1), 4)
            attn = plain_pieces(jnp.concatenate([attn, jnp.concatenate([vec] * HALVES)], axis=1))
            ff = plain_pieces(gather_plain(jnp.concatenate([w_up, w_down.T], axis=1), 2))
        qkvp, ho, hidden, vec, wa = attn_forward(place, frame_count, tokens, attn)
        if staged:
            ff = gather_last(ff, vec)
        mixed, gh, f_own, f_other, gv_two = feed_forward(
            place, live_count, hidden, cotangent, ho, vec, ff, out_dims
        )
        if staged:
            f_mine = scatter_core(f_own, f_other)
            gh = after(gh, *f_mine[1:])
            f_mine, f_got = scatter_plane(f_mine)
        grad_input, a_own, a_other = attn_backward(
            place, tokens, gh, qkvp, wa, vec, gv_two, out_dims
        )
        if staged:
            a_mine = scatter_core(a_own, a_other)
            f_mine = after(scatter_add(f_mine, f_got), *a_mine[1:])
            f_mine, f_got = scatter_z(f_mine)
            a_mine, a_got = scatter_plane(a_mine)
            a_mine = after(scatter_add(a_mine, a_got), *f_got)
            gf = scatter_sum(f_mine, f_got)
            ga = scatter_sum(*scatter_z(a_mine))
        else:
            gf = scatter_plain(f_own, f_other, (FW, FW, HW))
            ga = scatter_plain(a_own, a_other, (HW,) * 3)
        wide = w_query.shape[1]
        tall = w_up.shape[1]
        gains = ga[:, 3 * wide :]
        return (
            mixed,
            grad_input,
            ga[:, :wide],
            ga[:, wide : 2 * wide],
            ga[:, 2 * wide : 3 * wide],
            gf[:, 2 * tall :].T,
            gf[:, :tall],
            gf[:, tall : 2 * tall].T,
            gains[:, 0],
            gains[:, 1],
            gains[:, 2],
            gains[:, 3],
        )

    return shards


def solution(mesh):
    rows = P(("dp", "mp"), None)
    wide, tall, dp = P("dp", "mp"), P("mp", "dp"), P("dp")
    return jax.shard_map(
        build(mesh),
        mesh=mesh,
        in_specs=(rows, rows, dp, dp, wide, wide, wide, tall, wide, tall, dp, dp, dp, dp),
        out_specs=(rows, rows, wide, wide, wide, tall, wide, tall, dp, dp, dp, dp),
        check_vma=False,
    )
```

```python
import jax
import jax.numpy as jnp
from jax import lax
from jax.experimental import pallas as pl
from jax.experimental.pallas import tpu as pltpu
from jax.sharding import PartitionSpec as P

D = 512
FF = 2048
HEAD = 64
FTOK = 8
SEQ = 48
HALVES = 2
HW = D // HALVES
FW = FF // HALVES
PAIR = 2 * HEAD
GC = 128
EPS = 1e-05
CHUNK = 256
BF = jnp.bfloat16
F32 = jnp.float32


def nn(a, b):
    return lax.dot_general(a, b, (((1,), (0,)), ((), ())), preferred_element_type=F32)


def nt(a, b):
    return lax.dot_general(a, b, (((1,), (1,)), ((), ())), preferred_element_type=F32)


def tn(a, b):
    return lax.dot_general(a, b, (((0,), (0,)), ((), ())), preferred_element_type=F32)


def norm_parts(rows):
    mean = jnp.mean(rows, axis=-1, keepdims=True)
    centered = rows - mean
    spread = jnp.mean(centered * centered, axis=-1, keepdims=True)
    rstd = lax.rsqrt(spread + EPS)
    return centered * rstd, rstd


def norm_back(n, rstd, gain, gy):
    gg = gy * gain
    first = jnp.mean(gg, axis=-1, keepdims=True)
    second = jnp.mean(gg * n, axis=-1, keepdims=True)
    return rstd * (gg - first - n * second)


def fold_rows(value):
    return jnp.sum(value.reshape(value.shape[0] // 8, 8, value.shape[1]), axis=0)


def per_head(rows):
    width = rows.shape[1]
    lane = lax.broadcasted_iota(jnp.int32, rows.shape, 1) // HEAD
    pad = jnp.zeros((HEAD - SEQ, width), rows.dtype)
    parts = []
    for h in range(width // HEAD):
        parts.append(jnp.where(lane == h, rows, jnp.zeros_like(rows)))
        parts.append(pad)
    return jnp.concatenate(parts, axis=0)


def pair_blocks(product):
    lane = lax.broadcasted_iota(jnp.int32, (SEQ, PAIR), 1)
    return jnp.where(lane < HEAD, product[:SEQ], product[HEAD : HEAD + SEQ])


def head_rows(rows):
    lane = lax.broadcasted_iota(jnp.int32, rows.shape, 1)
    zero = jnp.zeros_like(rows)
    return jnp.concatenate([jnp.where(lane < HEAD, rows, zero), jnp.where(lane < HEAD, zero, rows)], axis=0)


def pair_scores(left, right):
    right = jnp.concatenate([right, jnp.zeros((HEAD - SEQ, right.shape[1]), right.dtype)], axis=0)
    both = nt(head_rows(left), right)
    return jnp.concatenate([both[:SEQ], both[SEQ:]], axis=1)


def seq_slice(s, c, width):
    return (slice(s * SEQ, (s + 1) * SEQ), slice(c * width, (c + 1) * width))


def block_place(place, cr, xr, yr, zr):
    z, x, c, y = place[0], place[1], place[2], place[3]
    z = lax.rem(z - zr + place[4], place[4])
    return (y ^ yr, z * 4 + (x ^ xr) * 2 + (c ^ cr))


def load_pieces(place, pieces, metas, dst, sems):
    copies = []
    for piece, meta in zip(pieces, metas):
        depth = piece.shape[0] // len(meta)
        n_dp = D // depth
        for b, rel in enumerate(meta):
            m, dp = block_place(place, *rel)
            row = pl.multiple_of((m * n_dp + dp) * depth, depth)
            copy = pltpu.make_async_copy(
                piece.at[pl.ds(b * depth, depth), :], dst.at[pl.ds(row, depth), :], sems.at[len(copies)]
            )
            copy.start()
            copies.append(copy)
    return copies


def wait_all(copies):
    for copy in copies:
        copy.wait()


def store_blocks(place, acc, start, own_ref, other_ref):
    slots, n_z, depth, width = own_ref.shape
    n_dp = n_z * 4
    for core in range(2):

        @pl.when(place[2] == core)
        def _():
            for m in range(HALVES):
                for dp in range(n_dp):
                    z, x, c = dp // 4, (dp // 2) % 2, dp % 2
                    slot = (place[1] ^ x) + 2 * (place[3] ^ m)
                    back = lax.rem(z - place[0] + n_z, n_z)
                    rows = slice(dp * depth, (dp + 1) * depth)
                    ref = own_ref if c == core else other_ref
                    ref[slot, back, :, start : start + acc.shape[2]] = acc[m, rows, :].astype(BF)


def pack_kernel(q_ref, k_ref, v_ref, o_ref, u_ref, d_ref, vec_ref, attn_ref, ff_ref):
    at = 0
    for ref in (q_ref, k_ref, v_ref, o_ref):
        attn_ref[:, at : at + ref.shape[1]] = ref[...]
        at += ref.shape[1]
    vec = jnp.concatenate([vec_ref[...].astype(F32), jnp.zeros((GC - 4, vec_ref.shape[1]), F32)], axis=0)
    attn_ref[:, at:] = vec.T.astype(BF)
    ff_ref[:, : u_ref.shape[1]] = u_ref[...]
    ff_ref[:, u_ref.shape[1] :] = d_ref[...]


def attn_forward_kernel(place, frames, metas, x_ref, *refs):
    n = len(metas)
    pieces = refs[:n]
    qkvp_ref, ho_ref, hidden_ref, vec_ref, w_ref, s_ref, sems = refs[n:]
    q_ref, k_ref, v_ref, p_ref = (qkvp_ref.at[:, i * D : (i + 1) * D] for i in range(4))
    step = pl.program_id(0)
    seqs = x_ref.shape[0] // SEQ

    @pl.when(step == 0)
    def _():
        wait_all(load_pieces(place, pieces, metas, w_ref, sems))
        vec_ref[...] = w_ref[:D, 4 * HW :].astype(F32).T[:8]

    x = x_ref[...].astype(F32)
    n, _ = norm_parts(x)
    normed = (n * vec_ref[0:1] + vec_ref[1:2]).astype(BF)
    for m in range(HALVES):
        cols = slice(m * HW, (m + 1) * HW)
        for i, ref in enumerate((q_ref, k_ref)):
            ref[:, cols] = nn(normed, w_ref[m * D : (m + 1) * D, i * HW : (i + 1) * HW]).astype(BF)
    for s in range(seqs):
        for c in range(D // PAIR):
            at = seq_slice(s, c, PAIR)
            s_ref[at] = pair_scores(k_ref[at], q_ref[at])
    for m in range(HALVES):
        v_ref[:, m * HW : (m + 1) * HW] = nn(normed, w_ref[m * D : (m + 1) * D, 2 * HW : 3 * HW]).astype(BF)
    key = lax.broadcasted_iota(jnp.int32, (SEQ, PAIR), 0)
    query = lax.broadcasted_iota(jnp.int32, (SEQ, PAIR), 1) % HEAD
    for s in range(seqs):
        allowed = (key <= query) & (key < frames[place[5] + step * seqs + s] * FTOK)
        for c in range(D // PAIR):
            at = seq_slice(s, c, PAIR)
            scores = jnp.where(allowed, s_ref[at] * HEAD**-0.5, -1000000000.0)
            expd = jnp.exp(scores - jnp.max(scores, axis=0, keepdims=True))
            p_ref[at] = (expd * (1.0 / jnp.sum(expd, axis=0, keepdims=True))).astype(BF)
    for s in range(seqs):
        for c in range(D // PAIR):
            at = seq_slice(s, c, PAIR)
            ho_ref[at] = pair_blocks(tn(p_ref[at], v_ref[at])).astype(BF)
    attended = nt(ho_ref[:, :HW], w_ref[:D, 3 * HW : 4 * HW]) + nt(ho_ref[:, HW:], w_ref[D:, 3 * HW : 4 * HW])
    hidden_ref[...] = x + attended


GELU_A = (2.0 / jnp.pi) ** 0.5
GELU_B = 0.044715


def feed_forward_kernel(place, live, metas, hidden_ref, cot_ref, ho_ref, vec_ref, *refs):
    n = len(metas)
    (
        mixed_ref, gh_ref, own_ref, other_ref, gv_ref,
        w_ref, accu_ref, accd_ref, acco_ref, gvacc_ref, act_ref, gup_ref, go_ref, sems,
    ) = refs[n:]
    step = pl.program_id(0)
    last = pl.num_programs(0) - 1
    rows = hidden_ref.shape[0]

    @pl.when(step == 0)
    def _():
        copies = load_pieces(place, refs[:n], metas, w_ref, sems)
        accu_ref[...] = jnp.zeros_like(accu_ref)
        accd_ref[...] = jnp.zeros_like(accd_ref)
        acco_ref[...] = jnp.zeros_like(acco_ref)
        gvacc_ref[...] = jnp.zeros_like(gvacc_ref)
        wait_all(copies)

    hidden = hidden_ref[...]
    n, rstd = norm_parts(hidden)
    normed = (n * vec_ref[2:3] + vec_ref[3:4]).astype(BF)
    row = lax.broadcasted_iota(jnp.int32, (rows, 1), 0) + step * rows
    go = jnp.where(row < (live[0] - place[5]) * SEQ, cot_ref[...].astype(F32), 0.0)
    go_ref[...] = go.astype(BF)
    for m in range(HALVES):
        for c in range(FW // CHUNK):
            depth = slice(m * D, (m + 1) * D)
            cols = slice(m * FW + c * CHUNK, m * FW + (c + 1) * CHUNK)
            up = nn(normed, w_ref[depth, c * CHUNK : (c + 1) * CHUNK])
            ga = nn(go_ref[...], w_ref[depth, FW + c * CHUNK : FW + (c + 1) * CHUNK])
            sq = up * up
            th = jnp.tanh(up * (GELU_A + (GELU_A * GELU_B) * sq))
            half = 0.5 + 0.5 * th
            act_ref[:, cols] = (up * half).astype(BF)
            slope = half + (0.5 * up) * (1.0 - th * th) * (GELU_A + (3.0 * GELU_A * GELU_B) * sq)
            gup_ref[:, cols] = (ga * slope).astype(BF)
    down = jnp.zeros((rows, D), F32)
    gy = jnp.zeros((rows, D), F32)
    for m in range(HALVES):
        cols = slice(m * FW, (m + 1) * FW)
        down += nt(act_ref[:, cols], w_ref[m * D : (m + 1) * D, FW:])
        gy += nt(gup_ref[:, cols], w_ref[m * D : (m + 1) * D, :FW])
        accu_ref[m] += tn(normed, gup_ref[:, cols])
        accd_ref[m] += tn(go_ref[...], act_ref[:, cols])
    mixed_ref[...] = (hidden + down).astype(BF)
    gh_ref[...] = (go + norm_back(n, rstd, vec_ref[2:3], gy)).astype(BF)
    for m in range(HALVES):
        acco_ref[m] += tn(gh_ref[...], ho_ref[:, m * HW : (m + 1) * HW])
    gvacc_ref[0] += fold_rows(gy * n)
    gvacc_ref[1] += fold_rows(gy)

    @pl.when(step == last)
    def _():
        store_blocks(place, accu_ref, 0, own_ref, other_ref)
        store_blocks(place, accd_ref, FW, own_ref, other_ref)
        store_blocks(place, acco_ref, 2 * FW, own_ref, other_ref)
        gv_ref[0:1] = jnp.sum(gvacc_ref[0], axis=0, keepdims=True)
        gv_ref[1:2] = jnp.sum(gvacc_ref[1], axis=0, keepdims=True)


def attn_backward_kernel(
    place, x_ref, gh_ref, qkvp_ref, w_ref, vec_ref, gvtwo_ref,
    gi_ref, own_ref, other_ref, acc_ref, gvacc_ref, gvec_ref, s_ref, ds_ref, dh_ref, dqkv_ref,
):
    step = pl.program_id(0)
    last = pl.num_programs(0) - 1
    seqs = x_ref.shape[0] // SEQ
    q_ref, k_ref, v_ref, p_ref = (qkvp_ref.at[:, i * D : (i + 1) * D] for i in range(4))

    @pl.when(step == 0)
    def _():
        acc_ref[...] = jnp.zeros_like(acc_ref)
        gvacc_ref[...] = jnp.zeros_like(gvacc_ref)

    for m in range(HALVES):
        dh_ref[:, m * HW : (m + 1) * HW] = nn(gh_ref[...], w_ref[m * D : (m + 1) * D, 3 * HW : 4 * HW]).astype(BF)
    for s in range(seqs):
        for c in range(D // PAIR):
            at = seq_slice(s, c, PAIR)
            base = 3 * HW * (c * PAIR // HW) + c * PAIR % HW
            s_ref[at] = pair_scores(v_ref[at], dh_ref[at])
            dqkv_ref[at[0], base + 2 * HW : base + 2 * HW + PAIR] = nn(p_ref[at], per_head(dh_ref[at])).astype(BF)
    for s in range(seqs):
        for c in range(D // PAIR):
            at = seq_slice(s, c, PAIR)
            probs = p_ref[at].astype(F32)
            gp = s_ref[at]
            delta = jnp.sum(probs * gp, axis=0, keepdims=True)
            ds_ref[at] = (probs * ((gp - delta) * HEAD**-0.5)).astype(BF)
    for s in range(seqs):
        for c in range(D // PAIR):
            at = seq_slice(s, c, PAIR)
            base = 3 * HW * (c * PAIR // HW) + c * PAIR % HW
            dqkv_ref[at[0], base + HW : base + HW + PAIR] = nn(ds_ref[at], per_head(q_ref[at])).astype(BF)
            dqkv_ref[at[0], base : base + PAIR] = pair_blocks(tn(ds_ref[at], k_ref[at])).astype(BF)
    n, rstd = norm_parts(x_ref[...].astype(F32))
    normed = (n * vec_ref[0:1] + vec_ref[1:2]).astype(BF)
    gy = jnp.zeros(x_ref.shape, F32)
    for m in range(HALVES):
        cols = slice(3 * HW * m, 3 * HW * (m + 1))
        gy += nt(dqkv_ref[:, cols], w_ref[m * D : (m + 1) * D, : 3 * HW])
        acc_ref[m] += tn(normed, dqkv_ref[:, cols])
    gi_ref[...] = gh_ref[...].astype(F32) + norm_back(n, rstd, vec_ref[0:1], gy)
    gvacc_ref[0] += fold_rows(gy * n)
    gvacc_ref[1] += fold_rows(gy)

    @pl.when(step == last)
    def _():
        store_blocks(place, acc_ref, 0, own_ref, other_ref)
        one = jnp.concatenate([jnp.sum(gvacc_ref[i], axis=0, keepdims=True) for i in range(2)], axis=0)
        rows = jnp.concatenate([one, gvtwo_ref[...], jnp.zeros((GC - 4, D), F32)], axis=0)
        for m in range(HALVES):
            gvec_ref[m] = rows.T
        store_blocks(place, gvec_ref, 3 * HW, own_ref, other_ref)


def step_rows(rows):
    return 16 * SEQ if rows % (16 * SEQ) == 0 else 8 * SEQ


def row_block(rows, width):
    return pl.BlockSpec((step_rows(rows), width), lambda i, *_: (i, 0))


def held(shape):
    return pl.BlockSpec(shape, lambda i, *_: (0,) * len(shape), pipeline_mode=pl.Buffered(1))


def shape(dims, dtype):
    return jax.ShapeDtypeStruct(dims, dtype)


def vmem(mib):
    return pltpu.CompilerParams(vmem_limit_bytes=mib * 1024 * 1024)


HBM = pl.BlockSpec(memory_space=pl.ANY)


def weight_dims(group):
    return (HALVES * D, group[0][0].shape[1])


def copy_sems(group):
    return pltpu.SemaphoreType.DMA((sum(len(meta) for meta in group[1]),))


def cost(flops, nbytes):
    return pl.CostEstimate(flops=flops, bytes_accessed=nbytes, transcendentals=0)


def pack(w_query, w_key, w_value, w_out, w_up, w_down, vec):
    depth = w_query.shape[0]
    return pl.pallas_call(
        pack_kernel,
        out_shape=[shape((depth, 4 * w_query.shape[1] + GC), BF), shape((depth, 2 * w_up.shape[1]), BF)],
        name="pack",
    )(w_query, w_key, w_value, w_out, w_up, w_down, vec)


def attn_forward(place, frames, tokens, group):
    rows = tokens.shape[0]
    dims = weight_dims(group)
    return pl.pallas_call(
        lambda place, frames, *refs: attn_forward_kernel(place, frames, group[1], *refs),
        grid_spec=pltpu.PrefetchScalarGridSpec(
            num_scalar_prefetch=2,
            grid=(rows // step_rows(rows),),
            in_specs=[row_block(rows, D)] + [HBM] * len(group[0]),
            out_specs=[row_block(rows, 4 * D), row_block(rows, D), row_block(rows, D), held((8, D)), held(dims)],
            scratch_shapes=[pltpu.VMEM((step_rows(rows), D), F32), copy_sems(group)],
        ),
        out_shape=[
            shape((rows, 4 * D), BF),
            shape((rows, D), BF),
            shape((rows, D), F32),
            shape((8, D), F32),
            shape(dims, BF),
        ],
        compiler_params=vmem(60),
        cost_estimate=cost(rows * D * D * 24, rows * D * 18),
        name="attn_forward",
    )(place, frames, tokens, *group[0])


def feed_forward(place, live, hidden, cotangent, ho, vec, group, out_dims):
    rows = hidden.shape[0]
    grads = out_dims + (2 * FW + HW,)
    dims = weight_dims(group)
    return pl.pallas_call(
        lambda place, live, *refs: feed_forward_kernel(place, live, group[1], *refs),
        grid_spec=pltpu.PrefetchScalarGridSpec(
            num_scalar_prefetch=2,
            grid=(rows // step_rows(rows),),
            in_specs=[row_block(rows, D)] * 3 + [held((8, D))] + [HBM] * len(group[0]),
            out_specs=[row_block(rows, D), row_block(rows, D), held(grads), held(grads), held((2, D))],
            scratch_shapes=[
                pltpu.VMEM(dims, BF),
                pltpu.VMEM((HALVES, D, FW), F32),
                pltpu.VMEM((HALVES, D, FW), F32),
                pltpu.VMEM((HALVES, D, HW), F32),
                pltpu.VMEM((2, 8, D), F32),
                pltpu.VMEM((step_rows(rows), FF), BF),
                pltpu.VMEM((step_rows(rows), FF), BF),
                pltpu.VMEM((step_rows(rows), D), BF),
                copy_sems(group),
            ],
        ),
        out_shape=[
            shape((rows, D), BF),
            shape((rows, D), BF),
            shape(grads, BF),
            shape(grads, BF),
            shape((2, D), F32),
        ],
        compiler_params=vmem(54),
        cost_estimate=cost(rows * D * FF * 12, rows * D * 12),
        name="feed_forward",
    )(place, live, hidden, cotangent, ho, vec, *group[0])


def attn_backward(place, tokens, gh, qkvp, w, vec, gv_two, out_dims):
    rows = tokens.shape[0]
    grads = out_dims + (3 * HW + GC,)
    return pl.pallas_call(
        attn_backward_kernel,
        grid_spec=pltpu.PrefetchScalarGridSpec(
            num_scalar_prefetch=1,
            grid=(rows // step_rows(rows),),
            in_specs=[row_block(rows, D)] * 2 + [row_block(rows, 4 * D), held(w.shape), held((8, D)), held((2, D))],
            out_specs=[row_block(rows, D), held(grads), held(grads)],
            scratch_shapes=[
                pltpu.VMEM((HALVES, D, 3 * HW), F32),
                pltpu.VMEM((2, 8, D), F32),
                pltpu.VMEM((HALVES, D, GC), F32),
                pltpu.VMEM((step_rows(rows), D), F32),
                pltpu.VMEM((step_rows(rows), D), BF),
                pltpu.VMEM((step_rows(rows), D), BF),
                pltpu.VMEM((step_rows(rows), 3 * D), BF),
            ],
        ),
        out_shape=[shape((rows, D), F32), shape(grads, BF), shape(grads, BF)],
        compiler_params=vmem(40),
        cost_estimate=cost(rows * D * D * 36, rows * D * 18),
        name="attn_backward",
    )(place, tokens, gh, qkvp, w, vec, gv_two)


def build(mesh):
    n_dp, n_mp = mesh.shape["dp"], mesh.shape["mp"]
    n_z = n_dp // 4
    depth = D // n_dp
    staged = n_mp == HALVES
    both = ("dp", "mp")
    PLANE = ((0, 0), (1, 0), (0, 1), (1, 1))

    def send(value, zr=0, xr=0, yr=0, cr=0):
        pairs = []
        for z in range(n_z):
            for x in range(2):
                for c in range(2):
                    for y in range(n_mp):
                        here = ((z * 2 + x) * 2 + c) * n_mp + y
                        there = ((((z + zr) % n_z) * 2 + (x ^ xr)) * 2 + (c ^ cr)) * n_mp + (y ^ yr)
                        pairs.append((here, there))
        return lax.ppermute(value, both, pairs)

    def along_z(value):
        return [value] + [send(value, zr=r) for r in range(1, n_z)]

    def across_plane(value):
        return [value] + [send(value, xr=x, yr=y) for x, y in PLANE[1:]]

    def both_cores(pieces):
        return pieces + [send(piece, cr=1) for piece in pieces]

    def stack(blocks):
        return jnp.concatenate(blocks, axis=0)

    Z_FIRST = tuple(tuple((c, x, y, z) for z in range(n_z)) for c in range(2) for x, y in PLANE)
    PLANE_FIRST = tuple(tuple((c, x, y, z) for x, y in PLANE) for c in range(2) for z in range(n_z))

    def after(value, *others):
        return lax.optimization_barrier((value,) + others)[0]

    def gather_first(attn, ff, place):
        attn_z = along_z(attn)
        attn_plane = across_plane(after(stack(attn_z), place))
        ff_z = along_z(after(ff, attn_z[-1]))
        ff_plane = across_plane(after(stack(ff_z), attn_plane[-1]))
        return (both_cores(attn_plane), Z_FIRST), ff_plane

    def gather_last(ff_plane, done):
        ff_plane = ff_plane[:1] + [after(piece, done) for piece in ff_plane[1:]]
        return both_cores(ff_plane), Z_FIRST

    def gather_plain(block, parts):
        out = lax.all_gather(block, ("mp", "dp"), axis=0, tiled=True)
        out = out.reshape(HALVES, n_mp // HALVES, D, parts, -1)
        return out.transpose(0, 2, 3, 1, 4).reshape(HALVES * D, -1)

    def plain_pieces(whole):
        z, x, c = lax.axis_index("dp") // 4, (lax.axis_index("dp") // 2) % 2, lax.axis_index("dp") % 2
        y = lax.axis_index("mp") % HALVES
        blocks = whole.reshape(HALVES, n_z, 2, 2, depth, -1)
        index = lambda n, at: (at - jnp.arange(n)) % n
        blocks = blocks[:, index(n_z, z)]
        blocks = blocks[y ^ jnp.arange(2)][:, :, x ^ jnp.arange(2)][:, :, :, c ^ jnp.arange(2)]
        blocks = blocks.transpose(3, 0, 2, 1, 4, 5).reshape(8, n_z * depth, -1)
        return [blocks[i] for i in range(8)], Z_FIRST

    def scatter_core(own, other):
        got = send(other, cr=1)
        return [(own[slot].astype(F32) + got[slot].astype(F32)).astype(BF) for slot in range(4)]

    def scatter_plane(mine):
        return mine[0], [send(mine[x + 2 * y], xr=x, yr=y) for x, y in PLANE[1:]]

    def scatter_add(mine, got):
        got = [part.astype(F32) for part in got]
        return ((mine.astype(F32) + got[0]) + (got[1] + got[2])).astype(BF)

    def scatter_z(mine):
        return mine[0], [send(mine[r], zr=r) for r in range(1, n_z)]

    def scatter_sum(mine, got):
        total = mine.astype(F32)
        for part in got:
            total += part.astype(F32)
        return total

    def scatter_plain(own, other, parts):
        z, x, c = lax.axis_index("dp") // 4, (lax.axis_index("dp") // 2) % 2, lax.axis_index("dp") % 2
        y = lax.axis_index("mp") % HALVES
        blocks = jnp.stack([own, other]).reshape(2, 2, 2, n_z, depth, -1)
        blocks = blocks[c ^ jnp.arange(2)][:, y ^ jnp.arange(2)][:, :, x ^ jnp.arange(2)]
        blocks = blocks[:, :, :, (jnp.arange(n_z) - z) % n_z]
        blocks = blocks.transpose(1, 3, 2, 0, 4, 5).reshape(HALVES, D, -1)
        main, start = [], 0
        for part in parts:
            cut = blocks[:, :, start : start + part].reshape(HALVES, D, n_mp // HALVES, -1)
            main.append(cut.transpose(0, 2, 1, 3).reshape(n_mp, D, -1))
            start += part
        main = jnp.concatenate(main, axis=2)
        tail = jnp.broadcast_to(blocks[:1, :, start:], (n_mp, D, blocks.shape[2] - start))
        flat = jnp.concatenate([main, tail], axis=2).reshape(n_mp * D, -1)
        return lax.psum_scatter(flat, ("mp", "dp"), scatter_dimension=0, tiled=True).astype(F32)

    def shards(
        tokens, cotangent, frame_count, live_count, w_query, w_key, w_value, w_out, w_up, w_down,
        gain_one, shift_one, gain_two, shift_two,
    ):
        dp, mp = lax.axis_index("dp"), lax.axis_index("mp")
        seqs = tokens.shape[0] // SEQ
        place = jnp.stack([dp // 4, (dp // 2) % 2, dp % 2, mp % HALVES, jnp.int32(n_z), mp * seqs])
        place = place.astype(jnp.int32)
        vec = jnp.stack([gain_one, shift_one, gain_two, shift_two])
        out_dims = (4, n_z, depth)
        if staged:
            attn, ff = gather_first(*pack(w_query, w_key, w_value, w_out.T, w_up, w_down.T, vec), place)
        else:
            vec = lax.all_gather(jnp.pad(vec.T, ((0, 0), (0, GC - 4))), "dp", axis=0, tiled=True)
            attn = gather_plain(jnp.concatenate([w_query, w_key, w_value, w_out.T], axis=1), 4)
            attn = plain_pieces(jnp.concatenate([attn, jnp.concatenate([vec] * HALVES)], axis=1))
            ff = plain_pieces(gather_plain(jnp.concatenate([w_up, w_down.T], axis=1), 2))
        qkvp, ho, hidden, vec, wa = attn_forward(place, frame_count, tokens, attn)
        if staged:
            ff = gather_last(ff, vec)
        mixed, gh, f_own, f_other, gv_two = feed_forward(
            place, live_count, hidden, cotangent, ho, vec, ff, out_dims
        )
        if staged:
            f_mine = scatter_core(f_own, f_other)
            gh = after(gh, *f_mine[1:])
            f_mine, f_got = scatter_plane(f_mine)
        grad_input, a_own, a_other = attn_backward(
            place, tokens, gh, qkvp, wa, vec, gv_two, out_dims
        )
        if staged:
            a_mine = scatter_core(a_own, a_other)
            f_mine = after(scatter_add(f_mine, f_got), *a_mine[1:])
            f_mine, f_got = scatter_z(f_mine)
            a_mine, a_got = scatter_plane(a_mine)
            a_mine = after(scatter_add(a_mine, a_got), *f_got)
            gf = scatter_sum(f_mine, f_got)
            ga = scatter_sum(*scatter_z(a_mine))
        else:
            gf = scatter_plain(f_own, f_other, (FW, FW, HW))
            ga = scatter_plain(a_own, a_other, (HW,) * 3)
        wide = w_query.shape[1]
        tall = w_up.shape[1]
        gains = ga[:, 3 * wide :]
        return (
            mixed,
            grad_input,
            ga[:, :wide],
            ga[:, wide : 2 * wide],
            ga[:, 2 * wide : 3 * wide],
            gf[:, 2 * tall :].T,
            gf[:, :tall],
            gf[:, tall : 2 * tall].T,
            gains[:, 0],
            gains[:, 1],
            gains[:, 2],
            gains[:, 3],
        )

    return shards


def solution(mesh):
    rows = P(("dp", "mp"), None)
    wide, tall, dp = P("dp", "mp"), P("mp", "dp"), P("dp")
    return jax.shard_map(
        build(mesh),
        mesh=mesh,
        in_specs=(rows, rows, dp, dp, wide, wide, wide, tall, wide, tall, dp, dp, dp, dp),
        out_specs=(rows, rows, wide, wide, wide, tall, wide, tall, dp, dp, dp, dp),
        check_vma=False,
    )
```

```python
import jax
import jax.numpy as jnp
from jax import lax
from jax.experimental import pallas as pl
from jax.experimental.pallas import tpu as pltpu
from jax.sharding import PartitionSpec as P

D = 512
FF = 2048
HEAD = 64
FTOK = 8
SEQ = 48
HALVES = 2
HW = D // HALVES
FW = FF // HALVES
PAIR = 2 * HEAD
GC = 128
EPS = 1e-05
CHUNK = 256
BF = jnp.bfloat16
F32 = jnp.float32


def nn(a, b):
    return lax.dot_general(a, b, (((1,), (0,)), ((), ())), preferred_element_type=F32)


def nt(a, b):
    return lax.dot_general(a, b, (((1,), (1,)), ((), ())), preferred_element_type=F32)


def tn(a, b):
    return lax.dot_general(a, b, (((0,), (0,)), ((), ())), preferred_element_type=F32)


def norm_parts(rows):
    mean = jnp.mean(rows, axis=-1, keepdims=True)
    centered = rows - mean
    spread = jnp.mean(centered * centered, axis=-1, keepdims=True)
    rstd = lax.rsqrt(spread + EPS)
    return centered * rstd, rstd


def norm_back(n, rstd, gain, gy):
    gg = gy * gain
    first = jnp.mean(gg, axis=-1, keepdims=True)
    second = jnp.mean(gg * n, axis=-1, keepdims=True)
    return rstd * (gg - first - n * second)


def fold_rows(value):
    return jnp.sum(value.reshape(value.shape[0] // 8, 8, value.shape[1]), axis=0)


def per_head(rows):
    width = rows.shape[1]
    lane = lax.broadcasted_iota(jnp.int32, rows.shape, 1) // HEAD
    pad = jnp.zeros((HEAD - SEQ, width), rows.dtype)
    parts = []
    for h in range(width // HEAD):
        parts.append(jnp.where(lane == h, rows, jnp.zeros_like(rows)))
        parts.append(pad)
    return jnp.concatenate(parts, axis=0)


def pair_blocks(product):
    lane = lax.broadcasted_iota(jnp.int32, (SEQ, PAIR), 1)
    return jnp.where(lane < HEAD, product[:SEQ], product[HEAD : HEAD + SEQ])


def head_rows(rows):
    lane = lax.broadcasted_iota(jnp.int32, rows.shape, 1)
    zero = jnp.zeros_like(rows)
    return jnp.concatenate([jnp.where(lane < HEAD, rows, zero), jnp.where(lane < HEAD, zero, rows)], axis=0)


def pair_scores(left, right):
    right = jnp.concatenate([right, jnp.zeros((HEAD - SEQ, right.shape[1]), right.dtype)], axis=0)
    both = nt(head_rows(left), right)
    return jnp.concatenate([both[:SEQ], both[SEQ:]], axis=1)


def seq_slice(s, c, width):
    return (slice(s * SEQ, (s + 1) * SEQ), slice(c * width, (c + 1) * width))


def block_place(place, cr, xr, yr, zr):
    z, x, c, y = place[0], place[1], place[2], place[3]
    z = lax.rem(z - zr + place[4], place[4])
    return (y ^ yr, z * 4 + (x ^ xr) * 2 + (c ^ cr))


def load_pieces(place, pieces, metas, dst, sems):
    copies = []
    for piece, meta in zip(pieces, metas):
        depth = piece.shape[0] // len(meta)
        n_dp = D // depth
        for b, rel in enumerate(meta):
            m, dp = block_place(place, *rel)
            row = pl.multiple_of((m * n_dp + dp) * depth, depth)
            copy = pltpu.make_async_copy(
                piece.at[pl.ds(b * depth, depth), :], dst.at[pl.ds(row, depth), :], sems.at[len(copies)]
            )
            copy.start()
            copies.append(copy)
    return copies


def wait_all(copies):
    for copy in copies:
        copy.wait()


def store_blocks(place, acc, start, own_ref, other_ref):
    slots, n_z, depth, width = own_ref.shape
    n_dp = n_z * 4
    for core in range(2):

        @pl.when(place[2] == core)
        def _():
            for m in range(HALVES):
                for dp in range(n_dp):
                    z, x, c = dp // 4, (dp // 2) % 2, dp % 2
                    slot = (place[1] ^ x) + 2 * (place[3] ^ m)
                    back = lax.rem(z - place[0] + n_z, n_z)
                    rows = slice(dp * depth, (dp + 1) * depth)
                    ref = own_ref if c == core else other_ref
                    ref[slot, back, :, start : start + acc.shape[2]] = acc[m, rows, :].astype(BF)


def pack_kernel(q_ref, k_ref, v_ref, o_ref, u_ref, d_ref, vec_ref, attn_ref, ff_ref):
    at = 0
    for ref in (q_ref, k_ref, v_ref, o_ref):
        attn_ref[:, at : at + ref.shape[1]] = ref[...]
        at += ref.shape[1]
    vec = jnp.concatenate([vec_ref[...].astype(F32), jnp.zeros((GC - 4, vec_ref.shape[1]), F32)], axis=0)
    attn_ref[:, at:] = vec.T.astype(BF)
    ff_ref[:, : u_ref.shape[1]] = u_ref[...]
    ff_ref[:, u_ref.shape[1] :] = d_ref[...]


def attn_forward_kernel(place, frames, metas, x_ref, *refs):
    n = len(metas)
    pieces = refs[:n]
    qkvp_ref, ho_ref, hidden_ref, vec_ref, w_ref, s_ref, sems = refs[n:]
    q_ref, k_ref, v_ref, p_ref = (qkvp_ref.at[:, i * D : (i + 1) * D] for i in range(4))
    step = pl.program_id(0)
    seqs = x_ref.shape[0] // SEQ

    @pl.when(step == 0)
    def _():
        wait_all(load_pieces(place, pieces, metas, w_ref, sems))
        vec_ref[...] = w_ref[:D, 4 * HW :].astype(F32).T[:8]

    x = x_ref[...].astype(F32)
    n, _ = norm_parts(x)
    normed = (n * vec_ref[0:1] + vec_ref[1:2]).astype(BF)
    for m in range(HALVES):
        cols = slice(m * HW, (m + 1) * HW)
        for i, ref in enumerate((q_ref, k_ref)):
            ref[:, cols] = nn(normed, w_ref[m * D : (m + 1) * D, i * HW : (i + 1) * HW]).astype(BF)
    for s in range(seqs):
        for c in range(D // PAIR):
            at = seq_slice(s, c, PAIR)
            s_ref[at] = pair_scores(k_ref[at], q_ref[at])
    for m in range(HALVES):
        v_ref[:, m * HW : (m + 1) * HW] = nn(normed, w_ref[m * D : (m + 1) * D, 2 * HW : 3 * HW]).astype(BF)
    key = lax.broadcasted_iota(jnp.int32, (SEQ, PAIR), 0)
    query = lax.broadcasted_iota(jnp.int32, (SEQ, PAIR), 1) % HEAD
    for s in range(seqs):
        allowed = (key <= query) & (key < frames[place[5] + step * seqs + s] * FTOK)
        for c in range(D // PAIR):
            at = seq_slice(s, c, PAIR)
            scores = jnp.where(allowed, s_ref[at] * HEAD**-0.5, -1000000000.0)
            expd = jnp.exp(scores - jnp.max(scores, axis=0, keepdims=True))
            p_ref[at] = (expd * (1.0 / jnp.sum(expd, axis=0, keepdims=True))).astype(BF)
    for s in range(seqs):
        for c in range(D // PAIR):
            at = seq_slice(s, c, PAIR)
            ho_ref[at] = pair_blocks(tn(p_ref[at], v_ref[at])).astype(BF)
    attended = nt(ho_ref[:, :HW], w_ref[:D, 3 * HW : 4 * HW]) + nt(ho_ref[:, HW:], w_ref[D:, 3 * HW : 4 * HW])
    hidden_ref[...] = x + attended


GELU_A = (2.0 / jnp.pi) ** 0.5
GELU_B = 0.044715


def feed_forward_kernel(place, live, metas, hidden_ref, cot_ref, ho_ref, vec_ref, *refs):
    n = len(metas)
    (
        mixed_ref, gh_ref, own_ref, other_ref, gv_ref,
        w_ref, accu_ref, accd_ref, acco_ref, gvacc_ref, act_ref, gup_ref, go_ref, sems,
    ) = refs[n:]
    step = pl.program_id(0)
    last = pl.num_programs(0) - 1
    rows = hidden_ref.shape[0]

    @pl.when(step == 0)
    def _():
        copies = load_pieces(place, refs[:n], metas, w_ref, sems)
        accu_ref[...] = jnp.zeros_like(accu_ref)
        accd_ref[...] = jnp.zeros_like(accd_ref)
        acco_ref[...] = jnp.zeros_like(acco_ref)
        gvacc_ref[...] = jnp.zeros_like(gvacc_ref)
        wait_all(copies)

    hidden = hidden_ref[...]
    n, rstd = norm_parts(hidden)
    normed = (n * vec_ref[2:3] + vec_ref[3:4]).astype(BF)
    row = lax.broadcasted_iota(jnp.int32, (rows, 1), 0) + step * rows
    go = jnp.where(row < (live[0] - place[5]) * SEQ, cot_ref[...].astype(F32), 0.0)
    go_ref[...] = go.astype(BF)
    for m in range(HALVES):
        for c in range(FW // CHUNK):
            depth = slice(m * D, (m + 1) * D)
            cols = slice(m * FW + c * CHUNK, m * FW + (c + 1) * CHUNK)
            up = nn(normed, w_ref[depth, c * CHUNK : (c + 1) * CHUNK])
            ga = nn(go_ref[...], w_ref[depth, FW + c * CHUNK : FW + (c + 1) * CHUNK])
            sq = up * up
            th = jnp.tanh(up * (GELU_A + (GELU_A * GELU_B) * sq))
            half = 0.5 + 0.5 * th
            act = up * half
            act_ref[:, cols] = act.astype(BF)
            slope = half + (act - act * half) * (2.0 * GELU_A + (6.0 * GELU_A * GELU_B) * sq)
            gup_ref[:, cols] = (ga * slope).astype(BF)
    down = jnp.zeros((rows, D), F32)
    gy = jnp.zeros((rows, D), F32)
    for m in range(HALVES):
        cols = slice(m * FW, (m + 1) * FW)
        down += nt(act_ref[:, cols], w_ref[m * D : (m + 1) * D, FW:])
        gy += nt(gup_ref[:, cols], w_ref[m * D : (m + 1) * D, :FW])
        accu_ref[m] += tn(normed, gup_ref[:, cols])
        accd_ref[m] += tn(go_ref[...], act_ref[:, cols])
    mixed_ref[...] = (hidden + down).astype(BF)
    gh_ref[...] = (go + norm_back(n, rstd, vec_ref[2:3], gy)).astype(BF)
    for m in range(HALVES):
        acco_ref[m] += tn(gh_ref[...], ho_ref[:, m * HW : (m + 1) * HW])
    gvacc_ref[0] += fold_rows(gy * n)
    gvacc_ref[1] += fold_rows(gy)

    @pl.when(step == last)
    def _():
        store_blocks(place, accu_ref, 0, own_ref, other_ref)
        store_blocks(place, accd_ref, FW, own_ref, other_ref)
        store_blocks(place, acco_ref, 2 * FW, own_ref, other_ref)
        gv_ref[0:1] = jnp.sum(gvacc_ref[0], axis=0, keepdims=True)
        gv_ref[1:2] = jnp.sum(gvacc_ref[1], axis=0, keepdims=True)


def attn_backward_kernel(
    place, x_ref, gh_ref, qkvp_ref, w_ref, vec_ref, gvtwo_ref,
    gi_ref, own_ref, other_ref, acc_ref, gvacc_ref, gvec_ref, s_ref, ds_ref, dh_ref, dqkv_ref,
):
    step = pl.program_id(0)
    last = pl.num_programs(0) - 1
    seqs = x_ref.shape[0] // SEQ
    q_ref, k_ref, v_ref, p_ref = (qkvp_ref.at[:, i * D : (i + 1) * D] for i in range(4))

    @pl.when(step == 0)
    def _():
        acc_ref[...] = jnp.zeros_like(acc_ref)
        gvacc_ref[...] = jnp.zeros_like(gvacc_ref)

    for m in range(HALVES):
        dh_ref[:, m * HW : (m + 1) * HW] = nn(gh_ref[...], w_ref[m * D : (m + 1) * D, 3 * HW : 4 * HW]).astype(BF)
    for s in range(seqs):
        for c in range(D // PAIR):
            at = seq_slice(s, c, PAIR)
            base = 3 * HW * (c * PAIR // HW) + c * PAIR % HW
            s_ref[at] = pair_scores(v_ref[at], dh_ref[at])
            dqkv_ref[at[0], base + 2 * HW : base + 2 * HW + PAIR] = nn(p_ref[at], per_head(dh_ref[at])).astype(BF)
    for s in range(seqs):
        for c in range(D // PAIR):
            at = seq_slice(s, c, PAIR)
            probs = p_ref[at].astype(F32)
            gp = s_ref[at]
            delta = jnp.sum(probs * gp, axis=0, keepdims=True)
            ds_ref[at] = (probs * ((gp - delta) * HEAD**-0.5)).astype(BF)
    for s in range(seqs):
        for c in range(D // PAIR):
            at = seq_slice(s, c, PAIR)
            base = 3 * HW * (c * PAIR // HW) + c * PAIR % HW
            dqkv_ref[at[0], base + HW : base + HW + PAIR] = nn(ds_ref[at], per_head(q_ref[at])).astype(BF)
            dqkv_ref[at[0], base : base + PAIR] = pair_blocks(tn(ds_ref[at], k_ref[at])).astype(BF)
    n, rstd = norm_parts(x_ref[...].astype(F32))
    normed = (n * vec_ref[0:1] + vec_ref[1:2]).astype(BF)
    gy = jnp.zeros(x_ref.shape, F32)
    for m in range(HALVES):
        cols = slice(3 * HW * m, 3 * HW * (m + 1))
        gy += nt(dqkv_ref[:, cols], w_ref[m * D : (m + 1) * D, : 3 * HW])
        acc_ref[m] += tn(normed, dqkv_ref[:, cols])
    gi_ref[...] = gh_ref[...].astype(F32) + norm_back(n, rstd, vec_ref[0:1], gy)
    gvacc_ref[0] += fold_rows(gy * n)
    gvacc_ref[1] += fold_rows(gy)

    @pl.when(step == last)
    def _():
        store_blocks(place, acc_ref, 0, own_ref, other_ref)
        one = jnp.concatenate([jnp.sum(gvacc_ref[i], axis=0, keepdims=True) for i in range(2)], axis=0)
        rows = jnp.concatenate([one, gvtwo_ref[...], jnp.zeros((GC - 4, D), F32)], axis=0)
        for m in range(HALVES):
            gvec_ref[m] = rows.T
        store_blocks(place, gvec_ref, 3 * HW, own_ref, other_ref)


def step_rows(rows):
    return 16 * SEQ if rows % (16 * SEQ) == 0 else 8 * SEQ


def row_block(rows, width):
    return pl.BlockSpec((step_rows(rows), width), lambda i, *_: (i, 0))


def held(shape):
    return pl.BlockSpec(shape, lambda i, *_: (0,) * len(shape), pipeline_mode=pl.Buffered(1))


def shape(dims, dtype):
    return jax.ShapeDtypeStruct(dims, dtype)


def vmem(mib):
    return pltpu.CompilerParams(vmem_limit_bytes=mib * 1024 * 1024)


HBM = pl.BlockSpec(memory_space=pl.ANY)


def weight_dims(group):
    return (HALVES * D, group[0][0].shape[1])


def copy_sems(group):
    return pltpu.SemaphoreType.DMA((sum(len(meta) for meta in group[1]),))


def cost(flops, nbytes):
    return pl.CostEstimate(flops=flops, bytes_accessed=nbytes, transcendentals=0)


def pack(w_query, w_key, w_value, w_out, w_up, w_down, vec):
    depth = w_query.shape[0]
    return pl.pallas_call(
        pack_kernel,
        out_shape=[shape((depth, 4 * w_query.shape[1] + GC), BF), shape((depth, 2 * w_up.shape[1]), BF)],
        name="pack",
    )(w_query, w_key, w_value, w_out, w_up, w_down, vec)


def attn_forward(place, frames, tokens, group):
    rows = tokens.shape[0]
    dims = weight_dims(group)
    return pl.pallas_call(
        lambda place, frames, *refs: attn_forward_kernel(place, frames, group[1], *refs),
        grid_spec=pltpu.PrefetchScalarGridSpec(
            num_scalar_prefetch=2,
            grid=(rows // step_rows(rows),),
            in_specs=[row_block(rows, D)] + [HBM] * len(group[0]),
            out_specs=[row_block(rows, 4 * D), row_block(rows, D), row_block(rows, D), held((8, D)), held(dims)],
            scratch_shapes=[pltpu.VMEM((step_rows(rows), D), F32), copy_sems(group)],
        ),
        out_shape=[
            shape((rows, 4 * D), BF),
            shape((rows, D), BF),
            shape((rows, D), F32),
            shape((8, D), F32),
            shape(dims, BF),
        ],
        compiler_params=vmem(60),
        cost_estimate=cost(rows * D * D * 24, rows * D * 18),
        name="attn_forward",
    )(place, frames, tokens, *group[0])


def feed_forward(place, live, hidden, cotangent, ho, vec, group, out_dims):
    rows = hidden.shape[0]
    grads = out_dims + (2 * FW + HW,)
    dims = weight_dims(group)
    return pl.pallas_call(
        lambda place, live, *refs: feed_forward_kernel(place, live, group[1], *refs),
        grid_spec=pltpu.PrefetchScalarGridSpec(
            num_scalar_prefetch=2,
            grid=(rows // step_rows(rows),),
            in_specs=[row_block(rows, D)] * 3 + [held((8, D))] + [HBM] * len(group[0]),
            out_specs=[row_block(rows, D), row_block(rows, D), held(grads), held(grads), held((2, D))],
            scratch_shapes=[
                pltpu.VMEM(dims, BF),
                pltpu.VMEM((HALVES, D, FW), F32),
                pltpu.VMEM((HALVES, D, FW), F32),
                pltpu.VMEM((HALVES, D, HW), F32),
                pltpu.VMEM((2, 8, D), F32),
                pltpu.VMEM((step_rows(rows), FF), BF),
                pltpu.VMEM((step_rows(rows), FF), BF),
                pltpu.VMEM((step_rows(rows), D), BF),
                copy_sems(group),
            ],
        ),
        out_shape=[
            shape((rows, D), BF),
            shape((rows, D), BF),
            shape(grads, BF),
            shape(grads, BF),
            shape((2, D), F32),
        ],
        compiler_params=vmem(54),
        cost_estimate=cost(rows * D * FF * 12, rows * D * 12),
        name="feed_forward",
    )(place, live, hidden, cotangent, ho, vec, *group[0])


def attn_backward(place, tokens, gh, qkvp, w, vec, gv_two, out_dims):
    rows = tokens.shape[0]
    grads = out_dims + (3 * HW + GC,)
    return pl.pallas_call(
        attn_backward_kernel,
        grid_spec=pltpu.PrefetchScalarGridSpec(
            num_scalar_prefetch=1,
            grid=(rows // step_rows(rows),),
            in_specs=[row_block(rows, D)] * 2 + [row_block(rows, 4 * D), held(w.shape), held((8, D)), held((2, D))],
            out_specs=[row_block(rows, D), held(grads), held(grads)],
            scratch_shapes=[
                pltpu.VMEM((HALVES, D, 3 * HW), F32),
                pltpu.VMEM((2, 8, D), F32),
                pltpu.VMEM((HALVES, D, GC), F32),
                pltpu.VMEM((step_rows(rows), D), F32),
                pltpu.VMEM((step_rows(rows), D), BF),
                pltpu.VMEM((step_rows(rows), D), BF),
                pltpu.VMEM((step_rows(rows), 3 * D), BF),
            ],
        ),
        out_shape=[shape((rows, D), F32), shape(grads, BF), shape(grads, BF)],
        compiler_params=vmem(40),
        cost_estimate=cost(rows * D * D * 36, rows * D * 18),
        name="attn_backward",
    )(place, tokens, gh, qkvp, w, vec, gv_two)


def build(mesh):
    n_dp, n_mp = mesh.shape["dp"], mesh.shape["mp"]
    n_z = n_dp // 4
    depth = D // n_dp
    staged = n_mp == HALVES
    both = ("dp", "mp")
    PLANE = ((0, 0), (1, 0), (0, 1), (1, 1))

    def send(value, zr=0, xr=0, yr=0, cr=0):
        pairs = []
        for z in range(n_z):
            for x in range(2):
                for c in range(2):
                    for y in range(n_mp):
                        here = ((z * 2 + x) * 2 + c) * n_mp + y
                        there = ((((z + zr) % n_z) * 2 + (x ^ xr)) * 2 + (c ^ cr)) * n_mp + (y ^ yr)
                        pairs.append((here, there))
        return lax.ppermute(value, both, pairs)

    def along_z(value):
        return [value] + [send(value, zr=r) for r in range(1, n_z)]

    def across_plane(value):
        return [value] + [send(value, xr=x, yr=y) for x, y in PLANE[1:]]

    def both_cores(pieces):
        return pieces + [send(piece, cr=1) for piece in pieces]

    def stack(blocks):
        return jnp.concatenate(blocks, axis=0)

    Z_FIRST = tuple(tuple((c, x, y, z) for z in range(n_z)) for c in range(2) for x, y in PLANE)
    PLANE_FIRST = tuple(tuple((c, x, y, z) for x, y in PLANE) for c in range(2) for z in range(n_z))

    def after(value, *others):
        return lax.optimization_barrier((value,) + others)[0]

    def gather_first(attn, ff, place):
        attn_z = along_z(attn)
        attn_plane = across_plane(after(stack(attn_z), place))
        ff_z = along_z(after(ff, attn_z[-1]))
        ff_plane = across_plane(after(stack(ff_z), attn_plane[-1]))
        return (both_cores(attn_plane), Z_FIRST), ff_plane

    def gather_last(ff_plane, done):
        ff_plane = ff_plane[:1] + [after(piece, done) for piece in ff_plane[1:]]
        return both_cores(ff_plane), Z_FIRST

    def gather_plain(block, parts):
        out = lax.all_gather(block, ("mp", "dp"), axis=0, tiled=True)
        out = out.reshape(HALVES, n_mp // HALVES, D, parts, -1)
        return out.transpose(0, 2, 3, 1, 4).reshape(HALVES * D, -1)

    def plain_pieces(whole):
        z, x, c = lax.axis_index("dp") // 4, (lax.axis_index("dp") // 2) % 2, lax.axis_index("dp") % 2
        y = lax.axis_index("mp") % HALVES
        blocks = whole.reshape(HALVES, n_z, 2, 2, depth, -1)
        index = lambda n, at: (at - jnp.arange(n)) % n
        blocks = blocks[:, index(n_z, z)]
        blocks = blocks[y ^ jnp.arange(2)][:, :, x ^ jnp.arange(2)][:, :, :, c ^ jnp.arange(2)]
        blocks = blocks.transpose(3, 0, 2, 1, 4, 5).reshape(8, n_z * depth, -1)
        return [blocks[i] for i in range(8)], Z_FIRST

    def scatter_core(own, other):
        got = send(other, cr=1)
        return [(own[slot].astype(F32) + got[slot].astype(F32)).astype(BF) for slot in range(4)]

    def scatter_plane(mine):
        return mine[0], [send(mine[x + 2 * y], xr=x, yr=y) for x, y in PLANE[1:]]

    def scatter_add(mine, got):
        got = [part.astype(F32) for part in got]
        return ((mine.astype(F32) + got[0]) + (got[1] + got[2])).astype(BF)

    def scatter_z(mine):
        return mine[0], [send(mine[r], zr=r) for r in range(1, n_z)]

    def scatter_sum(mine, got):
        total = mine.astype(F32)
        for part in got:
            total += part.astype(F32)
        return total

    def scatter_plain(own, other, parts):
        z, x, c = lax.axis_index("dp") // 4, (lax.axis_index("dp") // 2) % 2, lax.axis_index("dp") % 2
        y = lax.axis_index("mp") % HALVES
        blocks = jnp.stack([own, other]).reshape(2, 2, 2, n_z, depth, -1)
        blocks = blocks[c ^ jnp.arange(2)][:, y ^ jnp.arange(2)][:, :, x ^ jnp.arange(2)]
        blocks = blocks[:, :, :, (jnp.arange(n_z) - z) % n_z]
        blocks = blocks.transpose(1, 3, 2, 0, 4, 5).reshape(HALVES, D, -1)
        main, start = [], 0
        for part in parts:
            cut = blocks[:, :, start : start + part].reshape(HALVES, D, n_mp // HALVES, -1)
            main.append(cut.transpose(0, 2, 1, 3).reshape(n_mp, D, -1))
            start += part
        main = jnp.concatenate(main, axis=2)
        tail = jnp.broadcast_to(blocks[:1, :, start:], (n_mp, D, blocks.shape[2] - start))
        flat = jnp.concatenate([main, tail], axis=2).reshape(n_mp * D, -1)
        return lax.psum_scatter(flat, ("mp", "dp"), scatter_dimension=0, tiled=True).astype(F32)

    def shards(
        tokens, cotangent, frame_count, live_count, w_query, w_key, w_value, w_out, w_up, w_down,
        gain_one, shift_one, gain_two, shift_two,
    ):
        dp, mp = lax.axis_index("dp"), lax.axis_index("mp")
        seqs = tokens.shape[0] // SEQ
        place = jnp.stack([dp // 4, (dp // 2) % 2, dp % 2, mp % HALVES, jnp.int32(n_z), mp * seqs])
        place = place.astype(jnp.int32)
        vec = jnp.stack([gain_one, shift_one, gain_two, shift_two])
        out_dims = (4, n_z, depth)
        if staged:
            attn, ff = gather_first(*pack(w_query, w_key, w_value, w_out.T, w_up, w_down.T, vec), place)
        else:
            vec = lax.all_gather(jnp.pad(vec.T, ((0, 0), (0, GC - 4))), "dp", axis=0, tiled=True)
            attn = gather_plain(jnp.concatenate([w_query, w_key, w_value, w_out.T], axis=1), 4)
            attn = plain_pieces(jnp.concatenate([attn, jnp.concatenate([vec] * HALVES)], axis=1))
            ff = plain_pieces(gather_plain(jnp.concatenate([w_up, w_down.T], axis=1), 2))
        qkvp, ho, hidden, vec, wa = attn_forward(place, frame_count, tokens, attn)
        if staged:
            ff = gather_last(ff, vec)
        mixed, gh, f_own, f_other, gv_two = feed_forward(
            place, live_count, hidden, cotangent, ho, vec, ff, out_dims
        )
        if staged:
            f_mine = scatter_core(f_own, f_other)
            gh = after(gh, *f_mine[1:])
            f_mine, f_got = scatter_plane(f_mine)
        grad_input, a_own, a_other = attn_backward(
            place, tokens, gh, qkvp, wa, vec, gv_two, out_dims
        )
        if staged:
            a_mine = scatter_core(a_own, a_other)
            f_mine = after(scatter_add(f_mine, f_got), *a_mine[1:])
            f_mine, f_got = scatter_z(f_mine)
            a_mine, a_got = scatter_plane(a_mine)
            a_mine = after(scatter_add(a_mine, a_got), *f_got)
            gf = scatter_sum(f_mine, f_got)
            ga = scatter_sum(*scatter_z(a_mine))
        else:
            gf = scatter_plain(f_own, f_other, (FW, FW, HW))
            ga = scatter_plain(a_own, a_other, (HW,) * 3)
        wide = w_query.shape[1]
        tall = w_up.shape[1]
        gains = ga[:, 3 * wide :]
        return (
            mixed,
            grad_input,
            ga[:, :wide],
            ga[:, wide : 2 * wide],
            ga[:, 2 * wide : 3 * wide],
            gf[:, 2 * tall :].T,
            gf[:, :tall],
            gf[:, tall : 2 * tall].T,
            gains[:, 0],
            gains[:, 1],
            gains[:, 2],
            gains[:, 3],
        )

    return shards


def solution(mesh):
    rows = P(("dp", "mp"), None)
    wide, tall, dp = P("dp", "mp"), P("mp", "dp"), P("dp")
    return jax.shard_map(
        build(mesh),
        mesh=mesh,
        in_specs=(rows, rows, dp, dp, wide, wide, wide, tall, wide, tall, dp, dp, dp, dp),
        out_specs=(rows, rows, wide, wide, wide, tall, wide, tall, dp, dp, dp, dp),
        check_vma=False,
    )
```
